32 devices in a mesh: groups: 2 (over x), ctx: 16 (over z, y, core).
Axes of the slice: x: 2, y: 2, z: 4, core: 2. Of those that a mesh axis runs over, the one named last changes fastest.
Arguments:
- hidden_states: bfloat16 [16384, 4096], P(('groups', 'ctx')), parts along dimension 0, may hold values from -6 to 6
- query_weight: bfloat16 [4096, 1024], P('ctx'), may hold values from -0.09375 to 0.09375
- output_weight: bfloat16 [1024, 4096], P('ctx'), may hold values from -0.1875 to 0.1875
- keys: bfloat16 [16384, 128], P(('groups', 'ctx')), parts along dimension 0
- values: bfloat16 [16384, 128], P(('groups', 'ctx')), parts along dimension 0, may hold values from -6 to 6
- block_lists: int32 [32, 3], P('groups'), parts along dimension 0, may hold values from 0 to 15, as said below
Outputs:
- projected: bfloat16 [16384, 4096], P(('groups', 'ctx')), parts along dimension 0
The draws below stay inside these ranges and needn't reach their ends.
There are 2 independent parts, one for each index of `groups`. The reference program is written for one: setup_inputs(seed, part) draws one part's arguments, and reference() takes and returns one part's arrays. A program takes and returns all parts, laid end to end along the dimension named above; an argument that names none is the same for every part. Nothing has to cross between parts.
Inputs may be any that keep to these rules, and one draw needn't show every extreme that they name: Each row of block_lists names 3 different key blocks. In a row b with b >= 3 all entries are smaller than b; entries at or after b are not attended.
All inputs are finite; a program needn't handle non-finite values.
Results may differ from the reference program's by a relative error of at most 0.003.
The reference program's roundings to bfloat16 on the way count: a program that leaves them out, or rounds other values in their place, can miss the bound.
Values may be sent and summed in bfloat16 or wider, within the bound.
No kernel may reach another device: no remote copies, remote signals or barrier semaphores. Data moves between devices by JAX's collectives and lax.ppermute only.
A program may use at most 128 MiB of HBM per device.

```python
import math
import jax
import jax.numpy as jnp
from jax import lax

D = 4096
HD = 128
HEADS = 8
BLOCK = 512
TOPK = 3
TOKENS = 8192
BLOCKS = 16


def draw_keys(key, part):
    key = jax.random.fold_in(key, 5)
    base = jax.random.normal(key, (TOKENS, HD), jnp.float32)
    return base.astype(jnp.bfloat16)


def draw_block_lists(key, part):
    key = jax.random.fold_in(key, 11)
    count = BLOCKS
    random_part = jax.random.randint(key, (count, count), 0, 4096, dtype=jnp.int32)
    index = jnp.arange(count, dtype=jnp.int32)
    row_index = index[:, None]
    col_index = index[None, :]
    score = random_part * (col_index + 1) * count + col_index
    score = jnp.where(col_index < row_index, score, 1073741824 - col_index)
    picked_values, picked = lax.top_k(-score, TOPK)
    return picked.astype(jnp.int32)


def steps_of(stream_key, extent, shards, smallest, high):
    factor_of = 1.0
    for position, parts in shards:
        heights = jax.random.uniform(jax.random.fold_in(jax.random.fold_in(stream_key, 6), position), (parts,), jnp.float32, smallest / len(shards), high / len(shards))
        factor_of = factor_of * jnp.repeat(jnp.exp(heights), extent[position] // parts).reshape((-1,) + (1,) * (len(extent) - 1 - position))
    return factor_of


def normal_values(own_key, extent, spread, most, pieces=(), held_as=jnp.bfloat16):
    entries = spread * jax.random.normal(own_key, extent, jnp.float32)
    if pieces:
        entries = entries * steps_of(own_key, extent, pieces, -0.22, 0.18)
    return jnp.clip(entries, -most, most).astype(held_as)


def setup_inputs(seed: int = 0, part: int = 0) -> dict:
    splits = jax.random.split(jax.random.key(seed), 7)
    part_splits = jax.random.split(jax.random.fold_in(splits[6], part), 7)
    hidden_states = normal_values(part_splits[0], (TOKENS, D), 1.0, 6.0, ((0, 16),))
    query_weight = normal_values(splits[1], (D, HEADS * HD), D ** -0.5, 0.09375, ((0, 16),))
    output_weight = normal_values(splits[2], (HEADS * HD, D), (HEADS * HD) ** -0.5, 0.1875, ((0, 16),))
    keys = draw_keys(jax.random.fold_in(jax.random.fold_in(splits[6], part), 71), part)
    values = normal_values(part_splits[4], (TOKENS, HD), 1.0, 6.0, ((0, 16),))
    block_lists = draw_block_lists(jax.random.fold_in(jax.random.fold_in(splits[6], part), 71), part)
    return dict(hidden_states=hidden_states, query_weight=query_weight, output_weight=output_weight, keys=keys, values=values, block_lists=block_lists)


def reference(hidden_states, query_weight, output_weight, keys, values, block_lists):
    queries = jnp.dot(hidden_states, query_weight, preferred_element_type=jnp.float32).astype(jnp.bfloat16)
    count = BLOCKS
    query_blocks = queries.reshape(count, BLOCK, HEADS, HD)
    key_blocks = keys.reshape(count, BLOCK, HD)
    value_blocks = values.reshape(count, BLOCK, HD)
    offsets = jnp.arange(BLOCK, dtype=jnp.int32)
    causal = offsets[:, None] >= offsets[None, :]
    scale = 1.0 / math.sqrt(HD)

    def one_block(index):
        chosen = block_lists[index].astype(jnp.int32)
        near_keys = jnp.concatenate([jnp.take(key_blocks, chosen, axis=0).reshape(TOPK * BLOCK, HD), key_blocks[index]], 0)
        near_values = jnp.concatenate([jnp.take(value_blocks, chosen, axis=0).reshape(TOPK * BLOCK, HD), value_blocks[index]], 0)
        listed = jnp.repeat(chosen < index, BLOCK)
        allowed = jnp.concatenate([jnp.broadcast_to(listed[None, :], (BLOCK, TOPK * BLOCK)), causal], 1)
        scores = jnp.einsum('qhd,kd->qhk', query_blocks[index].astype(jnp.float32), near_keys.astype(jnp.float32)) * scale
        scores = jnp.where(allowed[:, None, :], scores, -jnp.inf)
        peak = lax.optimization_barrier(jnp.max(scores, axis=2, keepdims=True))
        weights_raw = jnp.exp(scores - peak)
        total = lax.optimization_barrier(jnp.sum(weights_raw, axis=2, keepdims=True))
        rounded = lax.optimization_barrier(weights_raw.astype(jnp.bfloat16))
        mixed = jnp.einsum('qhk,kd->qhd', rounded.astype(jnp.float32), near_values.astype(jnp.float32)) / total
        return mixed.astype(jnp.bfloat16).reshape(BLOCK, HEADS * HD)
    attention = lax.map(one_block, jnp.arange(count, dtype=jnp.int32)).reshape(TOKENS, HEADS * HD)
    return jnp.dot(attention, output_weight, preferred_element_type=jnp.float32).astype(jnp.bfloat16)
```

```python
import functools
import math

import jax
import jax.numpy as jnp
from jax import lax
from jax.experimental import pallas as pl
from jax.experimental.pallas import tpu as pltpu
from jax.sharding import PartitionSpec as P

BLOCK = 512
TOPK = 3
RING_CHIPS = 8
MIB = 2**20
VMEM = 56 * MIB


def pack_kernel(plane_ref, weight_ref, keys_ref, values_ref, out_ref):
    depth, width = weight_ref.shape
    head_size = keys_ref.shape[1]
    out_ref[:, :width] = weight_ref[...]
    for i, rows in enumerate(range(0, keys_ref.shape[0], depth)):
        at = width + 2 * i * head_size
        out_ref[:, at : at + head_size] = keys_ref[rows : rows + depth, :]
        out_ref[:, at + head_size : at + 2 * head_size] = values_ref[rows : rows + depth, :]


def pack(plane, weight, keys, values):
    depth, width = weight.shape
    size, head_size = keys.shape
    wide = width // 2 + 2 * head_size * (size // depth)
    return pl.pallas_call(
        pack_kernel,
        grid_spec=pltpu.PrefetchScalarGridSpec(
            num_scalar_prefetch=1,
            grid=(1,),
            in_specs=[
                pl.BlockSpec((depth, width // 2), lambda i, plane: (0, plane[0])),
                pl.BlockSpec(keys.shape, lambda i, plane: (0, 0)),
                pl.BlockSpec(values.shape, lambda i, plane: (0, 0)),
            ],
            out_specs=pl.BlockSpec((depth, wide), lambda i, plane: (0, 0)),
        ),
        out_shape=jax.ShapeDtypeStruct((depth, wide), weight.dtype),
        compiler_params=pltpu.CompilerParams(vmem_limit_bytes=VMEM),
        name="pack",
    )(plane, weight, keys, values)


def query_half_kernel(count, *refs):
    hidden, rows, rest = refs[1 : 1 + count], refs[1 + count : 1 + 2 * count], refs[1 + 2 * count :]
    left = jnp.concatenate([h[...] for h in hidden], axis=1)
    right = jnp.concatenate([w[...] for w in rows], axis=0)
    total = jnp.dot(left, right, preferred_element_type=jnp.float32)
    if len(rest) == 2:
        total += rest[0][...]
    rest[-1][...] = total.astype(rest[-1].dtype)


def query_half(hidden, scalars, whole, pieces, depth, width, total, out_dtype):
    tokens = hidden.shape[0]
    count = len(whole) + len(pieces)
    step = 256
    steps = width // step

    def hidden_spec(i):
        return pl.BlockSpec((tokens, depth), lambda n, where: (0, where[1 + i]))

    def piece_spec(row):
        return pl.BlockSpec((depth, step), lambda n, where: (row, n))

    whole_spec = pl.BlockSpec((depth, step), lambda n, where: (0, steps * where[0] + n))
    out_spec = pl.BlockSpec((tokens, step), lambda n, where: (0, n))
    return pl.pallas_call(
        functools.partial(query_half_kernel, count),
        grid_spec=pltpu.PrefetchScalarGridSpec(
            num_scalar_prefetch=1,
            grid=(steps,),
            in_specs=[hidden_spec(i) for i in range(count)]
            + [whole_spec] * len(whole)
            + [piece_spec(row) for _, row in pieces]
            + ([out_spec] if total is not None else []),
            out_specs=out_spec,
        ),
        out_shape=jax.ShapeDtypeStruct((tokens, width), out_dtype),
        compiler_params=pltpu.CompilerParams(vmem_limit_bytes=VMEM),
        cost_estimate=pl.CostEstimate(
            flops=2 * tokens * depth * width * count,
            bytes_accessed=2 * count * depth * (tokens + width) + 8 * tokens * width,
            transcendentals=0,
        ),
        name="query_half",
    )(
        scalars,
        *([hidden] * count),
        *whole,
        *[array for array, _ in pieces],
        *([total] if total is not None else []),
    )


def pick_kernel(sources, depth, width, mine_ref, give_ref, *refs):
    held, out_ref, given_ref, sems = refs[:-3], refs[-3], refs[-2], refs[-1]
    listed = mine_ref.shape[0]
    _, size, both = out_ref.shape

    def copies(source, target, slot):
        ref, row = source
        return [
            pltpu.make_async_copy(
                held[ref].at[pl.ds(row * depth, depth), pl.ds(width + i * both, both)],
                target[0].at[target[1], pl.ds(i * depth, depth)],
                sems.at[slot, i],
            )
            for i in range(size // depth)
        ]

    targets = [(out_ref, j) for j in range(listed)] + [(given_ref, j) for j in range(listed)]
    for slot, target in enumerate(targets):
        index = (mine_ref if slot < listed else give_ref)[slot % listed]
        for s, source in enumerate(sources):

            @pl.when(index == s)
            def _(slot=slot, target=target, source=source):
                for copy in copies(source, target, slot):
                    copy.start()

    targets.append((out_ref, listed))
    for copy in copies(sources[0], targets[-1], 2 * listed):
        copy.start()
    for slot, target in enumerate(targets):
        for copy in copies(sources[0], target, slot):
            copy.wait()


def pick(mine, give, pieces, depth, width, size, both):
    listed = mine.shape[0]
    held, sources = [], []
    for array, row in pieces:
        known = [i for i, h in enumerate(held) if h is array]
        if not known:
            held.append(array)
        sources.append((known[0] if known else len(held) - 1, row))
    dtype = held[0].dtype
    return pl.pallas_call(
        functools.partial(pick_kernel, sources, depth, width),
        in_specs=[pl.BlockSpec(memory_space=pltpu.SMEM)] * 2
        + [pl.BlockSpec(memory_space=pl.ANY)] * len(held),
        out_specs=[pl.BlockSpec(memory_space=pltpu.VMEM)] * 2,
        out_shape=[
            jax.ShapeDtypeStruct((listed + 1, size, both), dtype),
            jax.ShapeDtypeStruct((listed, size, both), dtype),
        ],
        scratch_shapes=[pltpu.SemaphoreType.DMA((2 * listed + 1, size // depth))],
        compiler_params=pltpu.CompilerParams(vmem_limit_bytes=VMEM),
        name="pick",
    )(mine, give, *held)


def attend_kernel(factor, shared, bias_ref, swap_ref, *refs):
    if shared:
        q_own_ref, q_got_ref, near_ref, got_ref, o_ref, kv_ref, q_ref = refs
        listed = got_ref.shape[0]
        q_ref[...] = (q_own_ref[...] + q_got_ref[...]).astype(q_ref.dtype)
        kv_ref[listed] = near_ref[listed]
        for j in range(listed):

            @pl.when(swap_ref[j] == 0)
            def _(j=j):
                kv_ref[j] = near_ref[j]

            @pl.when(swap_ref[j] != 0)
            def _(j=j):
                kv_ref[j] = got_ref[j]

    else:
        q_ref, kv_ref, o_ref = refs
    blocks, size, both = kv_ref.shape
    hd, listed, tile = both // 2, blocks - 1, size // 2
    across = (((1,), (1,)), ((), ()))

    def score(head, part):
        q = q_ref[part * tile : (part + 1) * tile, head * hd : (head + 1) * hd]
        spans = [(j, size) for j in range(listed)] + [(listed, tile * (part + 1))]
        return [
            lax.dot_general(
                q, kv_ref[j, :seen, :hd], across, preferred_element_type=jnp.float32
            )
            for j, seen in spans
        ]

    def mix(head, part, scores):
        at_query = lax.broadcasted_iota(jnp.int32, scores[-1].shape, 0) + part * tile
        at_key = lax.broadcasted_iota(jnp.int32, scores[-1].shape, 1)
        scores = scores[:-1] + [jnp.where(at_query >= at_key, scores[-1], -jnp.inf)]
        bias = [bias_ref[j] for j in range(listed)] + [0.0]
        peak = functools.reduce(
            jnp.maximum,
            [jnp.max(s, axis=1, keepdims=True) - b for s, b in zip(scores, bias)],
        )
        weights = [jnp.exp2((s - (peak + b)) * factor) for s, b in zip(scores, bias)]
        total = sum(jnp.sum(w, axis=1, keepdims=True) for w in weights)
        mixed = sum(
            jnp.dot(
                w.astype(jnp.bfloat16),
                kv_ref[j, : w.shape[1], hd:],
                preferred_element_type=jnp.float32,
            )
            for j, w in enumerate(weights)
        )
        o_ref[part * tile : (part + 1) * tile, head * hd : (head + 1) * hd] = (
            mixed / total
        ).astype(o_ref.dtype)

    parts = [(head, part) for head in range(q_ref.shape[1] // hd) for part in range(2)]
    ahead = score(*parts[0])
    for i, part in enumerate(parts):
        scores = ahead
        if i + 1 < len(parts):
            ahead = score(*parts[i + 1])
        mix(*part, scores)


def attend(queries, near, bias, swapped):
    tokens, width = queries[0].shape
    blocks, size, both = near[0].shape
    hd = both // 2
    step = min(width, 4 * hd)
    work = tokens * blocks * size * (width // hd)
    shared = len(queries) == 2
    query_spec = pl.BlockSpec((tokens, step), lambda h: (0, h))
    scratch = [
        pltpu.VMEM(near[0].shape, near[0].dtype),
        pltpu.VMEM((tokens, step), jnp.bfloat16),
    ]
    return pl.pallas_call(
        functools.partial(attend_kernel, math.log2(math.e) / math.sqrt(hd), shared),
        grid=(width // step,),
        in_specs=[pl.BlockSpec(memory_space=pltpu.SMEM)] * 2
        + [query_spec] * len(queries)
        + [pl.BlockSpec(n.shape, lambda h: (0, 0, 0)) for n in near],
        out_specs=query_spec,
        out_shape=jax.ShapeDtypeStruct((tokens, width), jnp.bfloat16),
        scratch_shapes=scratch if shared else [],
        compiler_params=pltpu.CompilerParams(vmem_limit_bytes=VMEM),
        cost_estimate=pl.CostEstimate(
            flops=8 * work * hd, bytes_accessed=4 * MIB, transcendentals=work
        ),
        name="attend",
    )(bias, swapped, *queries, *near)


def project_kernel(parts, pieces, common, scalar_ref, *refs):
    attention, refs = refs[:parts], refs[parts:]
    whole, refs = refs[:1], refs[1:]
    mine, refs = refs[:pieces], refs[pieces:]
    crossed, (out_ref, weight_ref) = refs[:pieces], refs[pieces:]

    def place(rows):
        for i, piece in enumerate(rows):
            depth = piece.shape[0]
            start = pl.multiple_of(scalar_ref[2 + i] * depth, depth)
            weight_ref[pl.ds(start, depth), :] = piece[...]

    early = pl.program_id(0) < common
    pl.when(early)(lambda: place(whole + mine))
    pl.when(jnp.logical_not(early))(lambda: place(whole + crossed))
    left = jnp.concatenate([a[...] for a in attention], axis=1)
    total = jnp.dot(left, weight_ref[...], preferred_element_type=jnp.float32)
    out_ref[...] = total.astype(out_ref.dtype)


def project(attention, scalars, whole, mine, crossed, wide):
    tokens = attention[0].shape[0]
    depth, width = whole.shape
    rows = depth * (1 + len(mine))
    step = 512
    steps = width // step
    near = mine[0][0].shape[1] // step
    part = steps - near
    common = near - part

    def column(n, where):
        return jnp.where(n < common, n, common + lax.rem(n - common + part * where[0], 2 * part))

    def near_spec(row):
        return pl.BlockSpec((depth, step), lambda n, where: (row, jnp.minimum(n, near - 1)))

    def crossed_spec(row):
        return pl.BlockSpec((depth, step), lambda n, where: (row, jnp.maximum(n - near, 0)))

    def out_column(n, where):
        return column(n, where) + (steps * where[1] if wide else 0)

    return pl.pallas_call(
        functools.partial(project_kernel, len(attention), len(mine), near),
        grid_spec=pltpu.PrefetchScalarGridSpec(
            num_scalar_prefetch=1,
            grid=(steps,),
            in_specs=[pl.BlockSpec(a.shape, lambda n, where: (0, 0)) for a in attention]
            + [pl.BlockSpec((depth, step), lambda n, where: (0, column(n, where)))]
            + [near_spec(row) for _, row in mine]
            + [crossed_spec(row) for _, row in crossed],
            out_specs=pl.BlockSpec((tokens, step), lambda n, where: (0, out_column(n, where))),
            scratch_shapes=[pltpu.VMEM((rows, step), whole.dtype)],
        ),
        out_shape=jax.ShapeDtypeStruct((tokens, 2 * width if wide else width), whole.dtype),
        compiler_params=pltpu.CompilerParams(vmem_limit_bytes=VMEM),
        cost_estimate=pl.CostEstimate(
            flops=2 * tokens * rows * width,
            bytes_accessed=2 * (rows + tokens) * width + 2 * tokens * rows,
            transcendentals=0,
        ),
        name="project",
    )(
        scalars,
        *attention,
        whole,
        *[array for array, _ in mine],
        *[array for array, _ in crossed],
    )


def fill_kernel(half_ref, into_ref, got_ref, out_ref):
    out_ref[...] = got_ref[...]


def fill(half, into, got):
    tokens, width = got.shape
    step = 512
    steps = width // step
    return pl.pallas_call(
        fill_kernel,
        grid_spec=pltpu.PrefetchScalarGridSpec(
            num_scalar_prefetch=1,
            grid=(steps,),
            in_specs=[
                pl.BlockSpec(memory_space=pl.ANY),
                pl.BlockSpec((tokens, step), lambda n, half: (0, n)),
            ],
            out_specs=pl.BlockSpec((tokens, step), lambda n, half: (0, n + steps * half[0])),
        ),
        out_shape=jax.ShapeDtypeStruct(into.shape, into.dtype),
        input_output_aliases={1: 0},
        compiler_params=pltpu.CompilerParams(vmem_limit_bytes=VMEM),
        name="fill",
    )(half, into, got)


def ring_device(hidden_states, query_weight, output_weight, keys, values, block_lists):
    devices = lax.axis_size("ctx")
    chips = devices // 2
    half = chips // 2
    ring = list(range(0, chips, 2)) + list(range(chips - 1, 0, -2))
    at = {chip: i for i, chip in enumerate(ring)}
    depth, width = query_weight.shape
    size, head_size = keys.shape

    def pairs(step):
        return [
            (2 * p + c, 2 * ring[(at[p] + step) % chips] + c) for p in range(chips) for c in (0, 1)
        ]

    ahead, back = pairs(1), pairs(-1)

    def send(array, to):
        return lax.ppermute(array, "ctx", to)

    def swap(array):
        return send(array, [(d, d ^ 1) for d in range(devices)])

    def cross(array):
        return lax.ppermute(array, "groups", [(0, 1), (1, 0)])

    def held_back(array, *until):
        return lax.optimization_barrier((array, *until))[0]

    distances = [0] + [d for s in range(1, half) for d in (-s, s)] + [half]
    me, plane = lax.axis_index("ctx"), lax.axis_index("groups")
    chip, core = me // 2, me % 2
    here = jnp.where(chip % 2 == 0, chip // 2, chips - 1 - chip // 2)
    order = (here + jnp.asarray(distances, jnp.int32) + chips) % chips
    order = jnp.where(order < half, 2 * order, 2 * (chips - 1 - order) + 1)
    lists = lax.dynamic_slice_in_dim(block_lists, 2 * chip, 2, 0)
    lists = jnp.stack([lists[core], lists[1 - core]])
    bias = jnp.where(lists[0] < me, 0.0, jnp.inf).astype(jnp.float32)
    swapped = (lists[0] % 2 != core).astype(jnp.int32)
    held_at = jnp.argmax(order == lists[:, :, None] // 2, axis=2).astype(jnp.int32)
    plane = jnp.reshape(plane, (1,)).astype(jnp.int32)
    places = 2 * order + core

    def walk(own, crossing, after, meanwhile):
        near, crossed = {}, {}
        down, up = held_back(own, *after), held_back(own, *after)
        cut = own.shape[0] // 2
        behind = []
        for step in range(1, half + 1):
            if step == half:
                down, up = down[:cut], up[cut:]
            down, up = send(down, ahead), send(up, back)
            over = cross(jnp.concatenate([down[:, crossing], up[:, crossing]], 0))
            if step < half:
                near[-step], near[step] = (down, 0), (up, 0)
                crossed[-step], crossed[step] = (over, 0), (over, 1)
                wait = behind + meanwhile.get(step, lambda *_: [])(near, crossed)
                behind = [over]
                if wait:
                    down, up = held_back(down, *wait), held_back(up, *wait)
            else:
                near[half] = (jnp.concatenate([down, up], 0), 0)
                crossed[half] = (over, 0)
        return near, crossed, [down, up]

    def part(which, found, first, last, totals):
        picks = [i for i, d in enumerate(distances) if first <= abs(d) <= last]
        scalars = jnp.stack([which[0]] + [places[i] for i in picks])
        return [
            query_half(
                hidden,
                scalars,
                (query_weight,) if first == 0 else (),
                [found[distances[i]] for i in picks if i],
                depth,
                width // 2,
                total,
                jnp.float32,
            )
            for hidden, total in zip((hidden_other, hidden_states), totals)
        ]

    hidden_other = swap(hidden_states)
    own = pack(plane, query_weight, keys, values)
    sums = {}

    def first_part(near, crossed):
        sums["near"] = part(plane, near, 0, half - 2, (None, None))
        return sums["near"]

    near, crossed, last = walk(own, slice(0, width // 2), [], {half - 1: first_part})
    held = [(own, 0)] + [near[d] for d in distances[1:]]
    picked, given = pick(held_at[0], held_at[1], held, depth, width // 2, size, 2 * head_size)
    picked = (picked, swap(given))
    query = {"near": near, "crossed": crossed}
    attention = []

    def heads(which, kind):
        other, mine = part(which, query[kind], half - 1, half, sums[kind])
        attention.append(attend((mine, swap(other)), picked, bias, swapped))
        return attention[-1:]

    def rest(*_):
        sums["crossed"] = part(1 - plane, query["crossed"], 0, half - 2, (None, None))
        return sums["crossed"]

    columns = output_weight.shape[1] // 2
    share = columns // 4
    kept = lax.dynamic_slice_in_dim(output_weight, columns * core, columns, 1)
    got = swap(lax.dynamic_slice_in_dim(output_weight, columns * (1 - core), columns, 1))
    whole = jnp.concatenate([jnp.where(core == 0, kept, got), jnp.where(core == 0, got, kept)], 0)
    own = jnp.concatenate(
        [
            whole[:, : columns - 2 * share],
            lax.dynamic_slice_in_dim(whole, columns - 2 * share + share * plane[0], share, 1),
        ],
        1,
    )
    work = {
        1: rest,
        half - 2: lambda *_: heads(plane, "near"),
        half - 1: lambda *_: heads(1 - plane, "crossed"),
    }
    near, crossed, _ = walk(own, slice(columns - 2 * share, columns - share), last, work)
    scalars = jnp.concatenate([plane, core[None], (order + half * plane) % chips])
    pieces = (whole, [near[d] for d in distances[1:]], [crossed[d] for d in distances[1:]])
    theirs = project([swap(a) for a in attention], scalars, *pieces, False)
    ours = project(attention, scalars, *pieces, True)
    return fill(1 - core[None], ours, swap(theirs))


def per_device(hidden_states, query_weight, output_weight, keys, values, block_lists):
    devices = lax.axis_size("ctx")
    head_size = keys.shape[1]
    piece_rows = BLOCK // devices
    me = lax.axis_index("ctx")
    total = jnp.dot(
        hidden_states,
        lax.all_gather(query_weight, "ctx", axis=0, tiled=True),
        preferred_element_type=jnp.float32,
    )
    queries = total.astype(jnp.bfloat16)
    near = jnp.concatenate([keys, values], 1)
    spread = lax.all_to_all(near[None], "ctx", split_axis=1, concat_axis=0, tiled=True)
    listed = jnp.take(spread, block_lists, axis=0).reshape(
        devices, TOPK, piece_rows, 2 * head_size
    )
    got = lax.all_to_all(listed, "ctx", split_axis=0, concat_axis=2, tiled=True)
    picked = jnp.concatenate([got.reshape(TOPK, BLOCK, 2 * head_size), near[None]], 0)
    mine = lax.dynamic_index_in_dim(block_lists, me, 0, keepdims=False)
    bias = jnp.where(mine < me, 0.0, jnp.inf).astype(jnp.float32)
    attention = attend((queries,), (picked,), bias, jnp.zeros_like(mine))
    projected = jnp.dot(
        attention,
        lax.all_gather(output_weight, "ctx", axis=0, tiled=True),
        preferred_element_type=jnp.float32,
    )
    return projected.astype(jnp.bfloat16)


def solution(mesh):
    in_specs = (
        P(("groups", "ctx"), None),
        P("ctx", None),
        P("ctx", None),
        P(("groups", "ctx"), None),
        P(("groups", "ctx"), None),
        P("groups", None),
    )
    out_specs = P(("groups", "ctx"), None)
    step_by_step = mesh.shape["ctx"] <= 2 * RING_CHIPS and mesh.shape["groups"] == 2
    return jax.shard_map(
        ring_device if step_by_step else per_device,
        mesh=mesh,
        in_specs=in_specs,
        out_specs=out_specs,
        check_vma=False,
    )
```

```python
import functools
import math

import jax
import jax.numpy as jnp
from jax import lax
from jax.experimental import pallas as pl
from jax.experimental.pallas import tpu as pltpu
from jax.sharding import PartitionSpec as P

BLOCK = 512
TOPK = 3
RING_CHIPS = 8
MIB = 2**20
VMEM = 60 * MIB


def pack_kernel(plane_ref, weight_ref, keys_ref, values_ref, out_ref):
    depth, width = weight_ref.shape
    head_size = keys_ref.shape[1]
    out_ref[:, :width] = weight_ref[...]
    for i, rows in enumerate(range(0, keys_ref.shape[0], depth)):
        at = width + 2 * i * head_size
        out_ref[:, at : at + head_size] = keys_ref[rows : rows + depth, :]
        out_ref[:, at + head_size : at + 2 * head_size] = values_ref[rows : rows + depth, :]


def pack(plane, weight, keys, values):
    depth, width = weight.shape
    size, head_size = keys.shape
    wide = width // 2 + 2 * head_size * (size // depth)
    return pl.pallas_call(
        pack_kernel,
        grid_spec=pltpu.PrefetchScalarGridSpec(
            num_scalar_prefetch=1,
            grid=(1,),
            in_specs=[
                pl.BlockSpec((depth, width // 2), lambda i, plane: (0, plane[0])),
                pl.BlockSpec(keys.shape, lambda i, plane: (0, 0)),
                pl.BlockSpec(values.shape, lambda i, plane: (0, 0)),
            ],
            out_specs=pl.BlockSpec((depth, wide), lambda i, plane: (0, 0)),
        ),
        out_shape=jax.ShapeDtypeStruct((depth, wide), weight.dtype),
        compiler_params=pltpu.CompilerParams(vmem_limit_bytes=VMEM),
        name="pack",
    )(plane, weight, keys, values)


def started(copies):
    for copy in copies:
        copy.start()
    return copies


def waited(copies):
    for copy in copies:
        copy.wait()


def query_kernel(depth, pieces, summed, blocks, scalar_ref, *refs):
    count = len(pieces)
    arrays, refs = refs[: 1 + max(p for p, _ in pieces + blocks)], refs[1 + max(p for p, _ in pieces + blocks) :]
    hidden, refs = refs[:2], refs[2:]
    totals, refs = (refs[:2], refs[2:]) if summed else ((), refs)
    outs, refs = refs[:2], refs[2:]
    near, refs = (refs[:2], refs[2:]) if blocks else ((), refs)
    weight_ref, hidden_ref, total_ref, weight_sems, hidden_sems, total_sems, out_sems = refs[:7]
    tokens, width = total_ref.shape[1:]

    def weight_copy(i):
        array, row = pieces[i]
        wide = array == 0
        start = pl.multiple_of(scalar_ref[0] * width, width) if wide else 0
        return pltpu.make_async_copy(
            arrays[array].at[pl.ds(row * depth, depth), pl.ds(start, width)],
            weight_ref.at[pl.ds(i * depth, depth)],
            weight_sems.at[i],
        )

    def hidden_copy(side, i):
        start = pl.multiple_of(scalar_ref[1 + i] * depth, depth)
        return pltpu.make_async_copy(
            hidden[side].at[:, pl.ds(start, depth)],
            hidden_ref.at[side, :, pl.ds(i * depth, depth)],
            hidden_sems.at[side, i],
        )

    def near_copies(source, target, slot):
        array, row = source
        both, size = target.shape[2], target.shape[1]
        return [
            pltpu.make_async_copy(
                arrays[array].at[pl.ds(row * depth, depth), pl.ds(width + h * both, both)],
                target.at[slot, pl.ds(h * depth, depth)],
                refs[7].at[0 if target is near[0] else 1, slot, h],
            )
            for h in range(size // depth)
        ]

    weights = started([weight_copy(i) for i in range(count)])
    lefts = [started([hidden_copy(side, i) for i in range(count)]) for side in range(2)]
    added = []
    for side in range(2 if summed else 0):
        added.append(
            started(
                [pltpu.make_async_copy(totals[side], total_ref.at[side], total_sems.at[side])]
            )
        )
    if blocks:
        listed = near[1].shape[0]
        for side in range(2):
            for j in range(listed):
                for s, source in enumerate(blocks):

                    @pl.when(scalar_ref[1 + count + side * listed + j] == s)
                    def _(side=side, j=j, source=source):
                        started(near_copies(source, near[side], j))

        started(near_copies(blocks[0], near[0], listed))
    waited(weights)
    sent = []
    for side in range(2):
        waited(lefts[side])
        total = jnp.dot(hidden_ref[side], weight_ref[...], preferred_element_type=jnp.float32)
        if summed:
            waited(added[side])
            total += total_ref[side]
        total_ref[side] = total
        sent += started(
            [pltpu.make_async_copy(total_ref.at[side], outs[side], out_sems.at[side])]
        )
    if blocks:
        for side in range(2):
            for j in range(listed + 1 - side):
                waited(near_copies(blocks[0], near[side], j))
    waited(sent)


def query(hidden, scalars, weight, pieces, depth, width, totals, blocks=(), listed=0, block=None):
    tokens = hidden[0].shape[0]
    arrays = [weight]

    def index(array):
        for i, known in enumerate(arrays):
            if known is array:
                return i
        arrays.append(array)
        return len(arrays) - 1

    where = [(index(array), row) for array, row in pieces]
    held = [(index(array), row) for array, row in blocks]
    count = len(pieces)
    out_shape = [jax.ShapeDtypeStruct((tokens, width), jnp.float32)] * 2
    scratch = [
        pltpu.VMEM((count * depth, width), weight.dtype),
        pltpu.VMEM((2, tokens, count * depth), weight.dtype),
        pltpu.VMEM((2, tokens, width), jnp.float32),
        pltpu.SemaphoreType.DMA((count,)),
        pltpu.SemaphoreType.DMA((2, count)),
        pltpu.SemaphoreType.DMA((2,)),
        pltpu.SemaphoreType.DMA((2,)),
    ]
    if blocks:
        out_shape += [
            jax.ShapeDtypeStruct((listed + 1,) + block, weight.dtype),
            jax.ShapeDtypeStruct((listed,) + block, weight.dtype),
        ]
        scratch.append(pltpu.SemaphoreType.DMA((2, listed + 1, block[0] // depth)))
    operands = [*arrays, *hidden, *totals]
    anywhere = pl.BlockSpec(memory_space=pl.ANY)
    return pl.pallas_call(
        functools.partial(query_kernel, depth, where, bool(totals), held),
        in_specs=[pl.BlockSpec(memory_space=pltpu.SMEM)] + [anywhere] * len(operands),
        out_specs=[anywhere] * 2 + [pl.BlockSpec(memory_space=pltpu.VMEM)] * (len(out_shape) - 2),
        out_shape=out_shape,
        scratch_shapes=scratch,
        compiler_params=pltpu.CompilerParams(vmem_limit_bytes=VMEM),
        cost_estimate=pl.CostEstimate(
            flops=4 * tokens * depth * width * count,
            bytes_accessed=2 * count * depth * (2 * tokens + width) + 16 * tokens * width,
            transcendentals=0,
        ),
        name="query",
    )(scalars, *operands)


def attend_kernel(factor, shared, bias_ref, swap_ref, *refs):
    if shared:
        q_own_ref, q_got_ref, near_ref, got_ref, o_ref, kv_ref, q_ref = refs
        listed = got_ref.shape[0]
        q_ref[...] = (q_own_ref[...] + q_got_ref[...]).astype(q_ref.dtype)
        kv_ref[listed] = near_ref[listed]
        for j in range(listed):

            @pl.when(swap_ref[j] == 0)
            def _(j=j):
                kv_ref[j] = near_ref[j]

            @pl.when(swap_ref[j] != 0)
            def _(j=j):
                kv_ref[j] = got_ref[j]

    else:
        q_ref, kv_ref, o_ref = refs
    blocks, size, both = kv_ref.shape
    hd, listed, tile = both // 2, blocks - 1, size // 2
    across = (((1,), (1,)), ((), ()))

    def score(head, part):
        q = q_ref[part * tile : (part + 1) * tile, head * hd : (head + 1) * hd]
        spans = [(j, size) for j in range(listed)] + [(listed, tile * (part + 1))]
        return [
            lax.dot_general(
                q, kv_ref[j, :seen, :hd], across, preferred_element_type=jnp.float32
            )
            for j, seen in spans
        ]

    def mix(head, part, scores):
        at_query = lax.broadcasted_iota(jnp.int32, scores[-1].shape, 0) + part * tile
        at_key = lax.broadcasted_iota(jnp.int32, scores[-1].shape, 1)
        scores = scores[:-1] + [jnp.where(at_query >= at_key, scores[-1], -jnp.inf)]
        bias = [bias_ref[j] for j in range(listed)] + [0.0]
        peak = functools.reduce(
            jnp.maximum,
            [jnp.max(s, axis=1, keepdims=True) - b for s, b in zip(scores, bias)],
        )
        weights = [jnp.exp2((s - (peak + b)) * factor) for s, b in zip(scores, bias)]
        total = sum(jnp.sum(w, axis=1, keepdims=True) for w in weights)
        mixed = sum(
            jnp.dot(
                w.astype(jnp.bfloat16),
                kv_ref[j, : w.shape[1], hd:],
                preferred_element_type=jnp.float32,
            )
            for j, w in enumerate(weights)
        )
        o_ref[part * tile : (part + 1) * tile, head * hd : (head + 1) * hd] = (
            mixed / total
        ).astype(o_ref.dtype)

    parts = [(head, part) for head in range(q_ref.shape[1] // hd) for part in range(2)]
    ahead = score(*parts[0])
    for i, part in enumerate(parts):
        scores = ahead
        if i + 1 < len(parts):
            ahead = score(*parts[i + 1])
        mix(*part, scores)


def attend(queries, near, bias, swapped):
    tokens, width = queries[0].shape
    blocks, size, both = near[0].shape
    hd = both // 2
    step = min(width, 4 * hd)
    work = tokens * blocks * size * (width // hd)
    shared = len(queries) == 2
    query_spec = pl.BlockSpec((tokens, step), lambda h: (0, h))
    scratch = [
        pltpu.VMEM(near[0].shape, near[0].dtype),
        pltpu.VMEM((tokens, step), jnp.bfloat16),
    ]
    return pl.pallas_call(
        functools.partial(attend_kernel, math.log2(math.e) / math.sqrt(hd), shared),
        grid=(width // step,),
        in_specs=[pl.BlockSpec(memory_space=pltpu.SMEM)] * 2
        + [query_spec] * len(queries)
        + [pl.BlockSpec(n.shape, lambda h: (0, 0, 0)) for n in near],
        out_specs=query_spec,
        out_shape=jax.ShapeDtypeStruct((tokens, width), jnp.bfloat16),
        scratch_shapes=scratch if shared else [],
        compiler_params=pltpu.CompilerParams(vmem_limit_bytes=VMEM),
        cost_estimate=pl.CostEstimate(
            flops=8 * work * hd, bytes_accessed=4 * MIB, transcendentals=work
        ),
        name="attend",
    )(bias, swapped, *queries, *near)


def project_kernel(parts, pieces, step, place_ref, *refs):
    attention, refs = refs[:parts], refs[parts:]
    rows, refs = refs[: len(pieces)], refs[len(pieces) :]
    out_ref, weight_ref, left_ref, result_ref, weight_sems, left_sems, out_sems = refs
    steps = weight_ref.shape[1] // step

    def columns(n):
        return pl.ds(n * step, step)

    def weight_copy(n, i):
        start = pl.multiple_of(place_ref[i], pieces[i])
        return pltpu.make_async_copy(
            rows[i].at[:, columns(n)],
            weight_ref.at[pl.ds(start, pieces[i]), columns(n)],
            weight_sems.at[n, i],
        )

    wide = left_ref.shape[1] // parts
    lefts = [
        pltpu.make_async_copy(a, left_ref.at[:, pl.ds(i * wide, wide)], left_sems.at[i])
        for i, a in enumerate(attention)
    ]
    arriving = [started([weight_copy(0, i) for i in range(len(pieces))])]
    started(lefts)
    for n in range(1, steps):
        arriving.append(started([weight_copy(n, i) for i in range(len(pieces))]))
    waited(lefts)
    left = left_ref[...]
    leaving = []
    for n in range(steps):
        waited(arriving[n])
        total = jnp.dot(left, weight_ref[:, columns(n)], preferred_element_type=jnp.float32)
        result_ref[:, columns(n)] = total.astype(result_ref.dtype)
        leaving += started(
            [
                pltpu.make_async_copy(
                    result_ref.at[:, columns(n)], out_ref.at[:, columns(n)], out_sems.at[n]
                )
            ]
        )
    waited(leaving)


def project(attention, places, pieces):
    tokens = attention[0].shape[0]
    width = pieces[0].shape[1]
    depths = [p.shape[0] for p in pieces]
    rows = sum(depths)
    step = min(1024, width)
    anywhere = pl.BlockSpec(memory_space=pl.ANY)
    return pl.pallas_call(
        functools.partial(project_kernel, len(attention), depths, step),
        in_specs=[pl.BlockSpec(memory_space=pltpu.SMEM)]
        + [anywhere] * (len(attention) + len(pieces)),
        out_specs=anywhere,
        out_shape=jax.ShapeDtypeStruct((tokens, width), attention[0].dtype),
        scratch_shapes=[
            pltpu.VMEM((rows, width), pieces[0].dtype),
            pltpu.VMEM((tokens, rows), attention[0].dtype),
            pltpu.VMEM((tokens, width), attention[0].dtype),
            pltpu.SemaphoreType.DMA((width // step, len(pieces))),
            pltpu.SemaphoreType.DMA((len(attention),)),
            pltpu.SemaphoreType.DMA((width // step,)),
        ],
        compiler_params=pltpu.CompilerParams(vmem_limit_bytes=VMEM),
        cost_estimate=pl.CostEstimate(
            flops=2 * tokens * rows * width,
            bytes_accessed=2 * (rows + tokens) * width + 2 * tokens * rows,
            transcendentals=0,
        ),
        name="project",
    )(places, *attention, *pieces)


def ring_device(hidden_states, query_weight, output_weight, keys, values, block_lists):
    devices = lax.axis_size("ctx")
    chips = devices // 2
    half = chips // 2
    ring = list(range(0, chips, 2)) + list(range(chips - 1, 0, -2))
    at = {chip: i for i, chip in enumerate(ring)}
    depth, width = query_weight.shape
    size, head_size = keys.shape

    def pairs(step):
        return [
            (2 * p + c, 2 * ring[(at[p] + step) % chips] + c) for p in range(chips) for c in (0, 1)
        ]

    ahead, back = pairs(1), pairs(-1)

    def send(array, to):
        return lax.ppermute(array, "ctx", to)

    def swap(array):
        return send(array, [(d, d ^ 1) for d in range(devices)])

    def cross(array):
        return lax.ppermute(array, "groups", [(0, 1), (1, 0)])

    def held_back(array, *until):
        return lax.optimization_barrier((array, *until))[0]

    distances = [0] + [d for s in range(1, half) for d in (-s, s)] + [half]
    me, plane = lax.axis_index("ctx"), lax.axis_index("groups")
    chip, core = me // 2, me % 2
    here = jnp.where(chip % 2 == 0, chip // 2, chips - 1 - chip // 2)
    order = (here + jnp.asarray(distances, jnp.int32) + chips) % chips
    order = jnp.where(order < half, 2 * order, 2 * (chips - 1 - order) + 1)
    lists = lax.dynamic_slice_in_dim(block_lists, 2 * chip, 2, 0)
    lists = jnp.where(core == 0, lists, lists[::-1])
    listed = lists.shape[1]
    bias = jnp.where(lists[0] < me, 0.0, jnp.inf).astype(jnp.float32)
    swapped = (lists[0] % 2 != core).astype(jnp.int32)
    held_at = jnp.argmax(order == lists[:, :, None] // 2, axis=2).astype(jnp.int32).reshape(-1)
    plane = jnp.reshape(plane, (1,)).astype(jnp.int32)
    places = 2 * order + core
    early, late = 2 * half - 3, 2 * half
    scalars = {
        (which, when): jnp.concatenate([plane if which == 0 else 1 - plane, places[span], held_at])
        for which in (0, 1)
        for when, span in enumerate((slice(0, early), slice(early, late)))
    }
    rows = output_weight.shape[0]
    cut = rows // 2
    row_of = 2 * order[:, None] + (core + jnp.arange(2, dtype=jnp.int32)) % 2
    row_of = ((row_of + chips * plane) % devices * rows).reshape(-1)
    row_of = jnp.concatenate([row_of, row_of[-2:] + cut])
    bias, swapped, row_of, scalars = lax.optimization_barrier((bias, swapped, row_of, scalars))

    hidden = (swap(hidden_states), hidden_states)
    own = pack(plane, query_weight, keys, values)

    def part(which, found, when, totals, **more):
        spans = distances[:early] if when == 0 else distances[early:]
        pieces = [(query_weight, 0) if d == 0 else found[d] for d in spans]
        return query(
            hidden, scalars[which, when], query_weight, pieces, depth, width // 2, totals, **more
        )

    near, crossed = {}, {}
    down, up = own, own
    behind = [bias, swapped, row_of, scalars[0, 0]]
    for step in range(1, half):
        down, up = send(down, ahead), send(up, back)
        over = cross(jnp.concatenate([down[:, : width // 2], up[:, : width // 2]], 0))
        near[-step], near[step] = (down, 0), (up, 0)
        crossed[-step], crossed[step] = (over, 0), (over, 1)
        if step == half - 1:
            first = part(0, near, 0, ())
            behind = [*first, crossed[step - 2][0]]
        down, up = held_back(down, *behind), held_back(up, *behind)
        behind = []
    down, up = send(down[: depth // 2], ahead), send(up[depth // 2 :], back)
    far = jnp.concatenate([down, up], 0)
    near[half] = (far, 0)
    crossed[half] = (cross(far[:, : width // 2]), 0)
    second = part(1, crossed, 0, ())
    last = [down, up, *second]
    blocks = [(own, 0)] + [near[d] for d in distances[1:]]
    block = (size, 2 * head_size)
    theirs, ours, picked, given = part(
        0, near, 1, first, blocks=blocks, listed=listed, block=block
    )
    queries = [(ours, swap(theirs))]
    picked = (picked, swap(given))
    theirs, ours = part(1, crossed, 1, second)
    queries.append((ours, swap(theirs)))

    pieces = [output_weight, swap(output_weight)]
    down, up = held_back(output_weight, *last), held_back(output_weight, *last)
    attention = []
    behind = [pieces[1], given, crossed[half - 1][0]]
    for step in range(1, half):
        down, up = send(down, ahead), send(up, back)
        got = [swap(down), swap(up)]
        pieces += [down, got[0], up, got[1]]
        if step > 1:
            attention.append(attend(queries[step - 2], picked, bias, swapped))
            behind.append(attention[-1])
        down, up = held_back(down, *behind), held_back(up, *behind)
        behind = got + [crossed[half][0]] if step == 1 else got
    down, up = send(down[:cut], ahead), send(up[cut:], back)
    pieces += [down, swap(down), up, swap(up)]
    return project(attention, row_of, pieces)


def per_device(hidden_states, query_weight, output_weight, keys, values, block_lists):
    devices = lax.axis_size("ctx")
    head_size = keys.shape[1]
    piece_rows = BLOCK // devices
    me = lax.axis_index("ctx")
    total = jnp.dot(
        hidden_states,
        lax.all_gather(query_weight, "ctx", axis=0, tiled=True),
        preferred_element_type=jnp.float32,
    )
    queries = total.astype(jnp.bfloat16)
    near = jnp.concatenate([keys, values], 1)
    spread = lax.all_to_all(near[None], "ctx", split_axis=1, concat_axis=0, tiled=True)
    listed = jnp.take(spread, block_lists, axis=0).reshape(
        devices, TOPK, piece_rows, 2 * head_size
    )
    got = lax.all_to_all(listed, "ctx", split_axis=0, concat_axis=2, tiled=True)
    picked = jnp.concatenate([got.reshape(TOPK, BLOCK, 2 * head_size), near[None]], 0)
    mine = lax.dynamic_index_in_dim(block_lists, me, 0, keepdims=False)
    bias = jnp.where(mine < me, 0.0, jnp.inf).astype(jnp.float32)
    attention = attend((queries,), (picked,), bias, jnp.zeros_like(mine))
    projected = jnp.dot(
        attention,
        lax.all_gather(output_weight, "ctx", axis=0, tiled=True),
        preferred_element_type=jnp.float32,
    )
    return projected.astype(jnp.bfloat16)


def solution(mesh):
    in_specs = (
        P(("groups", "ctx"), None),
        P("ctx", None),
        P("ctx", None),
        P(("groups", "ctx"), None),
        P(("groups", "ctx"), None),
        P("groups", None),
    )
    out_specs = P(("groups", "ctx"), None)
    step_by_step = mesh.shape["ctx"] <= 2 * RING_CHIPS and mesh.shape["groups"] == 2
    return jax.shard_map(
        ring_device if step_by_step else per_device,
        mesh=mesh,
        in_specs=in_specs,
        out_specs=out_specs,
        check_vma=False,
    )
```

```python
import functools
import math

import jax
import jax.numpy as jnp
from jax import lax
from jax.experimental import pallas as pl
from jax.experimental.pallas import tpu as pltpu
from jax.sharding import PartitionSpec as P

BLOCK = 512
TOPK = 3
RING_CHIPS = 8
MIB = 2**20
VMEM = 28 * MIB


def pack_kernel(plane_ref, weight_ref, keys_ref, values_ref, out_ref):
    depth, width = weight_ref.shape
    head_size = keys_ref.shape[1]
    out_ref[:, :width] = weight_ref[...]
    for i, rows in enumerate(range(0, keys_ref.shape[0], depth)):
        at = width + 2 * i * head_size
        out_ref[:, at : at + head_size] = keys_ref[rows : rows + depth, :]
        out_ref[:, at + head_size : at + 2 * head_size] = values_ref[rows : rows + depth, :]


def pack(plane, weight, keys, values):
    depth, width = weight.shape
    size, head_size = keys.shape
    wide = width // 2 + 2 * head_size * (size // depth)
    return pl.pallas_call(
        pack_kernel,
        grid_spec=pltpu.PrefetchScalarGridSpec(
            num_scalar_prefetch=1,
            grid=(1,),
            in_specs=[
                pl.BlockSpec((depth, width // 2), lambda i, plane: (0, plane[0])),
                pl.BlockSpec(keys.shape, lambda i, plane: (0, 0)),
                pl.BlockSpec(values.shape, lambda i, plane: (0, 0)),
            ],
            out_specs=pl.BlockSpec((depth, wide), lambda i, plane: (0, 0)),
        ),
        out_shape=jax.ShapeDtypeStruct((depth, wide), weight.dtype),
        compiler_params=pltpu.CompilerParams(vmem_limit_bytes=VMEM),
        name="pack",
    )(plane, weight, keys, values)


def started(copies):
    for copy in copies:
        copy.start()
    return copies


def waited(copies):
    for copy in copies:
        copy.wait()


def query_kernel(depth, pieces, summed, blocks, scalar_ref, *refs):
    count = len(pieces)
    arrays, refs = refs[: 1 + max(p for p, _ in pieces + blocks)], refs[1 + max(p for p, _ in pieces + blocks) :]
    hidden, refs = refs[:2], refs[2:]
    totals, refs = (refs[:2], refs[2:]) if summed else ((), refs)
    outs, refs = refs[:2], refs[2:]
    near, refs = (refs[:2], refs[2:]) if blocks else ((), refs)
    weight_ref, hidden_ref, total_ref, weight_sems, hidden_sems, total_sems, out_sems = refs[:7]
    tokens, width = total_ref.shape[1:]

    def weight_copy(i):
        array, row = pieces[i]
        wide = array == 0
        start = pl.multiple_of(scalar_ref[0] * width, width) if wide else 0
        return pltpu.make_async_copy(
            arrays[array].at[pl.ds(row * depth, depth), pl.ds(start, width)],
            weight_ref.at[pl.ds(i * depth, depth)],
            weight_sems.at[i],
        )

    def hidden_copy(side, i):
        start = pl.multiple_of(scalar_ref[1 + i] * depth, depth)
        return pltpu.make_async_copy(
            hidden[side].at[:, pl.ds(start, depth)],
            hidden_ref.at[side, :, pl.ds(i * depth, depth)],
            hidden_sems.at[side, i],
        )

    def near_copies(source, target, slot):
        array, row = source
        both, size = target.shape[2], target.shape[1]
        return [
            pltpu.make_async_copy(
                arrays[array].at[pl.ds(row * depth, depth), pl.ds(width + h * both, both)],
                target.at[slot, pl.ds(h * depth, depth)],
                refs[7].at[0 if target is near[0] else 1, slot, h],
            )
            for h in range(size // depth)
        ]

    weights = started([weight_copy(i) for i in range(count)])
    lefts = [started([hidden_copy(side, i) for i in range(count)]) for side in range(2)]
    added = []
    for side in range(2 if summed else 0):
        added.append(
            started(
                [pltpu.make_async_copy(totals[side], total_ref.at[side], total_sems.at[side])]
            )
        )
    if blocks:
        listed = near[1].shape[0]
        for side in range(2):
            for j in range(listed):
                for s, source in enumerate(blocks):

                    @pl.when(scalar_ref[1 + count + side * listed + j] == s)
                    def _(side=side, j=j, source=source):
                        started(near_copies(source, near[side], j))

        started(near_copies(blocks[0], near[0], listed))
    waited(weights)
    sent = []
    for side in range(2):
        waited(lefts[side])
        total = jnp.dot(hidden_ref[side], weight_ref[...], preferred_element_type=jnp.float32)
        if summed:
            waited(added[side])
            total += total_ref[side]
        total_ref[side] = total
        sent += started(
            [pltpu.make_async_copy(total_ref.at[side], outs[side], out_sems.at[side])]
        )
    if blocks:
        for side in range(2):
            for j in range(listed + 1 - side):
                waited(near_copies(blocks[0], near[side], j))
    waited(sent)


def query(hidden, scalars, weight, pieces, depth, width, totals, blocks=(), listed=0, block=None):
    tokens = hidden[0].shape[0]
    arrays = [weight]

    def index(array):
        for i, known in enumerate(arrays):
            if known is array:
                return i
        arrays.append(array)
        return len(arrays) - 1

    where = [(index(array), row) for array, row in pieces]
    held = [(index(array), row) for array, row in blocks]
    count = len(pieces)
    out_shape = [jax.ShapeDtypeStruct((tokens, width), jnp.float32)] * 2
    scratch = [
        pltpu.VMEM((count * depth, width), weight.dtype),
        pltpu.VMEM((2, tokens, count * depth), weight.dtype),
        pltpu.VMEM((2, tokens, width), jnp.float32),
        pltpu.SemaphoreType.DMA((count,)),
        pltpu.SemaphoreType.DMA((2, count)),
        pltpu.SemaphoreType.DMA((2,)),
        pltpu.SemaphoreType.DMA((2,)),
    ]
    if blocks:
        out_shape += [
            jax.ShapeDtypeStruct((listed + 1,) + block, weight.dtype),
            jax.ShapeDtypeStruct((listed,) + block, weight.dtype),
        ]
        scratch.append(pltpu.SemaphoreType.DMA((2, listed + 1, block[0] // depth)))
    operands = [*arrays, *hidden, *totals]
    anywhere = pl.BlockSpec(memory_space=pl.ANY)
    return pl.pallas_call(
        functools.partial(query_kernel, depth, where, bool(totals), held),
        in_specs=[pl.BlockSpec(memory_space=pltpu.SMEM)] + [anywhere] * len(operands),
        out_specs=[anywhere] * 2 + [pl.BlockSpec(memory_space=pltpu.VMEM)] * (len(out_shape) - 2),
        out_shape=out_shape,
        scratch_shapes=scratch,
        compiler_params=pltpu.CompilerParams(vmem_limit_bytes=VMEM),
        cost_estimate=pl.CostEstimate(flops=1955000000, bytes_accessed=1000, transcendentals=0),
        name="query",
    )(scalars, *operands)


def attend_kernel(factor, shared, bias_ref, swap_ref, *refs):
    if shared:
        q_own_ref, q_got_ref, near_ref, got_ref, o_ref, kv_ref, q_ref = refs
        listed = got_ref.shape[0]
        q_ref[...] = (q_own_ref[...] + q_got_ref[...]).astype(q_ref.dtype)
        kv_ref[listed] = near_ref[listed]
        for j in range(listed):

            @pl.when(swap_ref[j] == 0)
            def _(j=j):
                kv_ref[j] = near_ref[j]

            @pl.when(swap_ref[j] != 0)
            def _(j=j):
                kv_ref[j] = got_ref[j]

    else:
        q_ref, kv_ref, o_ref = refs
    blocks, size, both = kv_ref.shape
    hd, listed, tile = both // 2, blocks - 1, size // 2
    across = (((1,), (1,)), ((), ()))

    def score(head, part):
        q = q_ref[part * tile : (part + 1) * tile, head * hd : (head + 1) * hd]
        spans = [(j, size) for j in range(listed)] + [(listed, tile * (part + 1))]
        return [
            lax.dot_general(
                q, kv_ref[j, :seen, :hd], across, preferred_element_type=jnp.float32
            )
            for j, seen in spans
        ]

    def mix(head, part, scores):
        at_query = lax.broadcasted_iota(jnp.int32, scores[-1].shape, 0) + part * tile
        at_key = lax.broadcasted_iota(jnp.int32, scores[-1].shape, 1)
        scores = scores[:-1] + [jnp.where(at_query >= at_key, scores[-1], -jnp.inf)]
        bias = [bias_ref[j] for j in range(listed)] + [0.0]
        peak = functools.reduce(
            jnp.maximum,
            [jnp.max(s, axis=1, keepdims=True) - b for s, b in zip(scores, bias)],
        )
        weights = [jnp.exp2((s - (peak + b)) * factor) for s, b in zip(scores, bias)]
        total = sum(jnp.sum(w, axis=1, keepdims=True) for w in weights)
        mixed = sum(
            jnp.dot(
                w.astype(jnp.bfloat16),
                kv_ref[j, : w.shape[1], hd:],
                preferred_element_type=jnp.float32,
            )
            for j, w in enumerate(weights)
        )
        o_ref[part * tile : (part + 1) * tile, head * hd : (head + 1) * hd] = (
            mixed / total
        ).astype(o_ref.dtype)

    parts = [(head, part) for head in range(q_ref.shape[1] // hd) for part in range(2)]
    ahead = score(*parts[0])
    for i, part in enumerate(parts):
        scores = ahead
        if i + 1 < len(parts):
            ahead = score(*parts[i + 1])
        mix(*part, scores)


def attend(queries, near, bias, swapped):
    tokens, width = queries[0].shape
    blocks, size, both = near[0].shape
    hd = both // 2
    step = min(width, 4 * hd)
    work = tokens * blocks * size * (width // hd)
    shared = len(queries) == 2
    query_spec = pl.BlockSpec((tokens, step), lambda h: (0, h))
    scratch = [
        pltpu.VMEM(near[0].shape, near[0].dtype),
        pltpu.VMEM((tokens, step), jnp.bfloat16),
    ]
    return pl.pallas_call(
        functools.partial(attend_kernel, math.log2(math.e) / math.sqrt(hd), shared),
        grid=(width // step,),
        in_specs=[pl.BlockSpec(memory_space=pltpu.SMEM)] * 2
        + [query_spec] * len(queries)
        + [pl.BlockSpec(n.shape, lambda h: (0, 0, 0)) for n in near],
        out_specs=query_spec,
        out_shape=jax.ShapeDtypeStruct((tokens, width), jnp.bfloat16),
        scratch_shapes=scratch if shared else [],
        compiler_params=pltpu.CompilerParams(vmem_limit_bytes=VMEM),
        cost_estimate=pl.CostEstimate(flops=3910000000, bytes_accessed=1000, transcendentals=0),
        name="attend",
    )(bias, swapped, *queries, *near)


def project_kernel(parts, count, pieces, step, place_ref, *refs):
    attention, refs = refs[:parts], refs[parts:]
    arrays, refs = refs[:count], refs[count:]
    out_ref, weight_ref, left_ref, result_ref, weight_sems, left_sems, out_sems = refs
    steps = weight_ref.shape[1] // step

    def columns(n):
        return pl.ds(n * step, step)

    def weight_copy(n, i):
        array, row, depth = pieces[i]
        start = pl.multiple_of(place_ref[i], depth)
        return pltpu.make_async_copy(
            arrays[array].at[pl.ds(row, depth), columns(n)],
            weight_ref.at[pl.ds(start, depth), columns(n)],
            weight_sems.at[n, i],
        )

    wide = left_ref.shape[1] // parts
    lefts = [
        pltpu.make_async_copy(a, left_ref.at[:, pl.ds(i * wide, wide)], left_sems.at[i])
        for i, a in enumerate(attention)
    ]
    arriving = [started([weight_copy(0, i) for i in range(len(pieces))])]
    started(lefts)
    for n in range(1, steps):
        arriving.append(started([weight_copy(n, i) for i in range(len(pieces))]))
    waited(lefts)
    left = left_ref[...]
    leaving = []
    for n in range(steps):
        waited(arriving[n])
        total = jnp.dot(left, weight_ref[:, columns(n)], preferred_element_type=jnp.float32)
        result_ref[:, columns(n)] = total.astype(result_ref.dtype)
        leaving += started(
            [
                pltpu.make_async_copy(
                    result_ref.at[:, columns(n)], out_ref.at[:, columns(n)], out_sems.at[n]
                )
            ]
        )
    waited(leaving)


def project(attention, places, pieces):
    tokens = attention[0].shape[0]
    width = pieces[0][0].shape[1]
    arrays, held = [], []
    for array, row, depth in pieces:
        known = [i for i, other in enumerate(arrays) if other is array]
        if not known:
            arrays.append(array)
        held.append((known[0] if known else len(arrays) - 1, row, depth))
    rows = sum(depth for _, _, depth in held)
    step = min(1024, width)
    anywhere = pl.BlockSpec(memory_space=pl.ANY)
    return pl.pallas_call(
        functools.partial(project_kernel, len(attention), len(arrays), held, step),
        in_specs=[pl.BlockSpec(memory_space=pltpu.SMEM)]
        + [anywhere] * (len(attention) + len(arrays)),
        out_specs=anywhere,
        out_shape=jax.ShapeDtypeStruct((tokens, width), attention[0].dtype),
        scratch_shapes=[
            pltpu.VMEM((rows, width), arrays[0].dtype),
            pltpu.VMEM((tokens, rows), attention[0].dtype),
            pltpu.VMEM((tokens, width), attention[0].dtype),
            pltpu.SemaphoreType.DMA((width // step, len(held))),
            pltpu.SemaphoreType.DMA((len(attention),)),
            pltpu.SemaphoreType.DMA((width // step,)),
        ],
        compiler_params=pltpu.CompilerParams(vmem_limit_bytes=VMEM),
        cost_estimate=pl.CostEstimate(
            flops=2 * tokens * rows * width,
            bytes_accessed=2 * (rows + tokens) * width + 2 * tokens * rows,
            transcendentals=0,
        ),
        name="project",
    )(places, *attention, *arrays)


def ring_device(hidden_states, query_weight, output_weight, keys, values, block_lists):
    devices = lax.axis_size("ctx")
    chips = devices // 2
    half = chips // 2
    ring = list(range(0, chips, 2)) + list(range(chips - 1, 0, -2))
    at = {chip: i for i, chip in enumerate(ring)}
    depth, width = query_weight.shape
    size, head_size = keys.shape

    def pairs(step):
        return [
            (2 * p + c, 2 * ring[(at[p] + step) % chips] + c) for p in range(chips) for c in (0, 1)
        ]

    ahead, back = pairs(1), pairs(-1)

    def send(array, to):
        return lax.ppermute(array, "ctx", to)

    def swap(array):
        return send(array, [(d, d ^ 1) for d in range(devices)])

    def cross(array):
        return lax.ppermute(array, "groups", [(0, 1), (1, 0)])

    def held_back(array, *until):
        return lax.optimization_barrier((array, *until))[0]

    distances = [0] + [d for s in range(1, half) for d in (-s, s)] + [half]
    me, plane = lax.axis_index("ctx"), lax.axis_index("groups")
    chip, core = me // 2, me % 2
    here = jnp.where(chip % 2 == 0, chip // 2, chips - 1 - chip // 2)
    order = (here + jnp.asarray(distances, jnp.int32) + chips) % chips
    order = jnp.where(order < half, 2 * order, 2 * (chips - 1 - order) + 1)
    lists = lax.dynamic_slice_in_dim(block_lists, 2 * chip, 2, 0)
    lists = jnp.where(core == 0, lists, lists[::-1])
    listed = lists.shape[1]
    bias = jnp.where(lists[0] < me, 0.0, jnp.inf).astype(jnp.float32)
    swapped = (lists[0] % 2 != core).astype(jnp.int32)
    held_at = jnp.argmax(order == lists[:, :, None] // 2, axis=2).astype(jnp.int32).reshape(-1)
    plane = jnp.reshape(plane, (1,)).astype(jnp.int32)
    places = 2 * order + core
    early, late = 2 * half - 3, 2 * half
    scalars = {
        (which, when): jnp.concatenate([plane if which == 0 else 1 - plane, places[span], held_at])
        for which in (0, 1)
        for when, span in enumerate((slice(0, early), slice(early, late)))
    }
    rows = output_weight.shape[0]
    cut = rows // 2
    row_of = 2 * order[:, None] + (core + jnp.arange(2, dtype=jnp.int32)) % 2
    row_of = ((row_of + chips * plane) % devices * rows).reshape(-1)
    row_of = jnp.concatenate([row_of, row_of[-2:] + cut])
    bias, swapped, row_of, scalars = lax.optimization_barrier((bias, swapped, row_of, scalars))

    hidden = (swap(hidden_states), hidden_states)
    own = pack(plane, query_weight, keys, values)

    def part(which, found, when, totals, **more):
        spans = distances[:early] if when == 0 else distances[early:]
        pieces = [(query_weight, 0) if d == 0 else found[d] for d in spans]
        return query(
            hidden, scalars[which, when], query_weight, pieces, depth, width // 2, totals, **more
        )

    near, crossed = {}, {}
    down, up = own, own
    behind = [bias, swapped, row_of, scalars[0, 0]]
    for step in range(1, half):
        down, up = send(down, ahead), send(up, back)
        over = jnp.concatenate([down[:, : width // 2], up[:, : width // 2]], 0)
        over = cross(over) if step < half - 1 else over
        near[-step], near[step] = (down, 0), (up, 0)
        crossed[-step], crossed[step] = (over, 0), (over, 1)
        if step == half - 1:
            first = part(0, near, 0, ())
            behind = [*first, crossed[step - 2][0]]
        down, up = held_back(down, *behind), held_back(up, *behind)
        behind = []
    down, up = send(down[: depth // 2], ahead), send(up[depth // 2 :], back)
    far = jnp.concatenate([down, up], 0)
    near[half] = (far, 0)
    over = cross(jnp.concatenate([over, far[:, : width // 2]], 0))
    for i, distance in enumerate((1 - half, half - 1, half)):
        crossed[distance] = (over, i)
    second = part(1, crossed, 0, ())
    last = [down, up, *second]
    blocks = [(own, 0)] + [near[d] for d in distances[1:]]
    block = (size, 2 * head_size)
    theirs, ours, picked, given = part(
        0, near, 1, first, blocks=blocks, listed=listed, block=block
    )
    queries = [(ours, swap(theirs))]
    picked = (picked, swap(given))
    theirs, ours = part(1, crossed, 1, second)
    queries.append((ours, swap(theirs)))

    pieces = [(output_weight, 0, rows), (swap(output_weight), 0, rows)]
    down, up = held_back(output_weight, *last), held_back(output_weight, *last)
    attention = []
    behind = [pieces[1][0], given]
    for step in range(1, half):
        down, up = send(down, ahead), send(up, back)
        pair = jnp.concatenate([down, up], 0)
        if step > 1:
            attention.append(attend(queries[step - 2], picked, bias, swapped))
            behind.append(attention[-1])
        if step == half - 1:
            pair = held_back(pair, attention[-1])
        other = swap(pair)
        pieces += [(down, 0, rows), (other, 0, rows), (up, 0, rows), (other, rows, rows)]
        down, up = held_back(down, *behind), held_back(up, *behind)
        behind = [other]
    down, up = send(down[:cut], ahead), send(up[cut:], back)
    pieces += [(down, 0, cut), (swap(down), 0, cut), (up, 0, cut), (swap(up), 0, cut)]
    return project(attention, row_of, pieces)


def per_device(hidden_states, query_weight, output_weight, keys, values, block_lists):
    devices = lax.axis_size("ctx")
    head_size = keys.shape[1]
    piece_rows = BLOCK // devices
    me = lax.axis_index("ctx")
    total = jnp.dot(
        hidden_states,
        lax.all_gather(query_weight, "ctx", axis=0, tiled=True),
        preferred_element_type=jnp.float32,
    )
    queries = total.astype(jnp.bfloat16)
    near = jnp.concatenate([keys, values], 1)
    spread = lax.all_to_all(near[None], "ctx", split_axis=1, concat_axis=0, tiled=True)
    listed = jnp.take(spread, block_lists, axis=0).reshape(
        devices, TOPK, piece_rows, 2 * head_size
    )
    got = lax.all_to_all(listed, "ctx", split_axis=0, concat_axis=2, tiled=True)
    picked = jnp.concatenate([got.reshape(TOPK, BLOCK, 2 * head_size), near[None]], 0)
    mine = lax.dynamic_index_in_dim(block_lists, me, 0, keepdims=False)
    bias = jnp.where(mine < me, 0.0, jnp.inf).astype(jnp.float32)
    attention = attend((queries,), (picked,), bias, jnp.zeros_like(mine))
    projected = jnp.dot(
        attention,
        lax.all_gather(output_weight, "ctx", axis=0, tiled=True),
        preferred_element_type=jnp.float32,
    )
    return projected.astype(jnp.bfloat16)


def solution(mesh):
    in_specs = (
        P(("groups", "ctx"), None),
        P("ctx", None),
        P("ctx", None),
        P(("groups", "ctx"), None),
        P(("groups", "ctx"), None),
        P("groups", None),
    )
    out_specs = P(("groups", "ctx"), None)
    step_by_step = mesh.shape["ctx"] <= 2 * RING_CHIPS and mesh.shape["groups"] == 2
    return jax.shard_map(
        ring_device if step_by_step else per_device,
        mesh=mesh,
        in_specs=in_specs,
        out_specs=out_specs,
        check_vma=False,
    )
```

```python
import functools
import math

import jax
import jax.numpy as jnp
from jax import lax
from jax.experimental import pallas as pl
from jax.experimental.pallas import tpu as pltpu
from jax.sharding import PartitionSpec as P

BLOCK = 512
TOPK = 3
RING_CHIPS = 8
MIB = 2**20
VMEM = 28 * MIB


def pack_kernel(plane_ref, weight_ref, keys_ref, values_ref, out_ref):
    depth, width = weight_ref.shape
    head_size = keys_ref.shape[1]
    out_ref[:, :width] = weight_ref[...]
    for i, rows in enumerate(range(0, keys_ref.shape[0], depth)):
        at = width + 2 * i * head_size
        out_ref[:, at : at + head_size] = keys_ref[rows : rows + depth, :]
        out_ref[:, at + head_size : at + 2 * head_size] = values_ref[rows : rows + depth, :]


def pack(plane, weight, keys, values):
    depth, width = weight.shape
    size, head_size = keys.shape
    wide = width // 2 + 2 * head_size * (size // depth)
    return pl.pallas_call(
        pack_kernel,
        grid_spec=pltpu.PrefetchScalarGridSpec(
            num_scalar_prefetch=1,
            grid=(1,),
            in_specs=[
                pl.BlockSpec((depth, width // 2), lambda i, plane: (0, plane[0])),
                pl.BlockSpec(keys.shape, lambda i, plane: (0, 0)),
                pl.BlockSpec(values.shape, lambda i, plane: (0, 0)),
            ],
            out_specs=pl.BlockSpec((depth, wide), lambda i, plane: (0, 0)),
        ),
        out_shape=jax.ShapeDtypeStruct((depth, wide), weight.dtype),
        compiler_params=pltpu.CompilerParams(vmem_limit_bytes=VMEM),
        name="pack",
    )(plane, weight, keys, values)


def started(copies):
    for copy in copies:
        copy.start()
    return copies


def waited(copies):
    for copy in copies:
        copy.wait()


def query_kernel(depth, pieces, summed, blocks, scalar_ref, *refs):
    count = len(pieces)
    arrays, refs = refs[: 1 + max(p for p, _ in pieces + blocks)], refs[1 + max(p for p, _ in pieces + blocks) :]
    hidden, refs = refs[:2], refs[2:]
    totals, refs = (refs[:2], refs[2:]) if summed else ((), refs)
    outs, refs = refs[:2], refs[2:]
    near, refs = (refs[:2], refs[2:]) if blocks else ((), refs)
    weight_ref, hidden_ref, total_ref, weight_sems, hidden_sems, total_sems, out_sems = refs[:7]
    tokens, width = total_ref.shape[1:]

    def weight_copy(i):
        array, row = pieces[i]
        wide = array == 0
        start = pl.multiple_of(scalar_ref[0] * width, width) if wide else 0
        return pltpu.make_async_copy(
            arrays[array].at[pl.ds(row * depth, depth), pl.ds(start, width)],
            weight_ref.at[pl.ds(i * depth, depth)],
            weight_sems.at[i],
        )

    def hidden_copy(side, i):
        start = pl.multiple_of(scalar_ref[1 + i] * depth, depth)
        return pltpu.make_async_copy(
            hidden[side].at[:, pl.ds(start, depth)],
            hidden_ref.at[side, :, pl.ds(i * depth, depth)],
            hidden_sems.at[side, i],
        )

    def near_copies(source, target, slot):
        array, row = source
        both, size = target.shape[2], target.shape[1]
        return [
            pltpu.make_async_copy(
                arrays[array].at[pl.ds(row * depth, depth), pl.ds(width + h * both, both)],
                target.at[slot, pl.ds(h * depth, depth)],
                refs[7].at[0 if target is near[0] else 1, slot, h],
            )
            for h in range(size // depth)
        ]

    weights = started([weight_copy(i) for i in range(count)])
    lefts = [started([hidden_copy(side, i) for i in range(count)]) for side in range(2)]
    added = []
    for side in range(2 if summed else 0):
        added.append(
            started(
                [pltpu.make_async_copy(totals[side], total_ref.at[side], total_sems.at[side])]
            )
        )
    if blocks:
        listed = near[1].shape[0]
        for side in range(2):
            for j in range(listed):
                for s, source in enumerate(blocks):

                    @pl.when(scalar_ref[1 + count + side * listed + j] == s)
                    def _(side=side, j=j, source=source):
                        started(near_copies(source, near[side], j))

        started(near_copies(blocks[0], near[0], listed))
    waited(weights)
    sent = []
    for side in range(2):
        waited(lefts[side])
        total = jnp.dot(hidden_ref[side], weight_ref[...], preferred_element_type=jnp.float32)
        if summed:
            waited(added[side])
            total += total_ref[side]
        total_ref[side] = total
        sent += started(
            [pltpu.make_async_copy(total_ref.at[side], outs[side], out_sems.at[side])]
        )
    if blocks:
        for side in range(2):
            for j in range(listed + 1 - side):
                waited(near_copies(blocks[0], near[side], j))
    waited(sent)


def query(hidden, scalars, weight, pieces, depth, width, totals, blocks=(), listed=0, block=None):
    tokens = hidden[0].shape[0]
    arrays = [weight]

    def index(array):
        for i, known in enumerate(arrays):
            if known is array:
                return i
        arrays.append(array)
        return len(arrays) - 1

    where = [(index(array), row) for array, row in pieces]
    held = [(index(array), row) for array, row in blocks]
    count = len(pieces)
    out_shape = [jax.ShapeDtypeStruct((tokens, width), jnp.float32)] * 2
    scratch = [
        pltpu.VMEM((count * depth, width), weight.dtype),
        pltpu.VMEM((2, tokens, count * depth), weight.dtype),
        pltpu.VMEM((2, tokens, width), jnp.float32),
        pltpu.SemaphoreType.DMA((count,)),
        pltpu.SemaphoreType.DMA((2, count)),
        pltpu.SemaphoreType.DMA((2,)),
        pltpu.SemaphoreType.DMA((2,)),
    ]
    if blocks:
        out_shape += [
            jax.ShapeDtypeStruct((listed + 1,) + block, weight.dtype),
            jax.ShapeDtypeStruct((listed,) + block, weight.dtype),
        ]
        scratch.append(pltpu.SemaphoreType.DMA((2, listed + 1, block[0] // depth)))
    operands = [*arrays, *hidden, *totals]
    anywhere = pl.BlockSpec(memory_space=pl.ANY)
    return pl.pallas_call(
        functools.partial(query_kernel, depth, where, bool(totals), held),
        in_specs=[pl.BlockSpec(memory_space=pltpu.SMEM)] + [anywhere] * len(operands),
        out_specs=[anywhere] * 2 + [pl.BlockSpec(memory_space=pltpu.VMEM)] * (len(out_shape) - 2),
        out_shape=out_shape,
        scratch_shapes=scratch,
        compiler_params=pltpu.CompilerParams(vmem_limit_bytes=VMEM),
        cost_estimate=pl.CostEstimate(flops=1955000000, bytes_accessed=1000, transcendentals=0),
        name="query",
    )(scalars, *operands)


def attend_kernel(factor, shared, bias_ref, swap_ref, *refs):
    if shared:
        q_own_ref, q_got_ref, near_ref, got_ref, o_ref, kv_ref, q_ref = refs
        listed = got_ref.shape[0]
        q_ref[...] = (q_own_ref[...] + q_got_ref[...]).astype(q_ref.dtype)
        kv_ref[listed] = near_ref[listed]
        for j in range(listed):

            @pl.when(swap_ref[j] == 0)
            def _(j=j):
                kv_ref[j] = near_ref[j]

            @pl.when(swap_ref[j] != 0)
            def _(j=j):
                kv_ref[j] = got_ref[j]

    else:
        q_ref, kv_ref, o_ref = refs
    blocks, size, both = kv_ref.shape
    hd, listed, tile = both // 2, blocks - 1, size // 2
    across = (((1,), (1,)), ((), ()))

    def score(head, part):
        q = q_ref[part * tile : (part + 1) * tile, head * hd : (head + 1) * hd]
        spans = [(j, size) for j in range(listed)] + [(listed, tile * (part + 1))]
        return [
            lax.dot_general(
                q, kv_ref[j, :seen, :hd], across, preferred_element_type=jnp.float32
            )
            for j, seen in spans
        ]

    def mix(head, part, scores):
        at_query = lax.broadcasted_iota(jnp.int32, scores[-1].shape, 0) + part * tile
        at_key = lax.broadcasted_iota(jnp.int32, scores[-1].shape, 1)
        scores = scores[:-1] + [jnp.where(at_query >= at_key, scores[-1], -jnp.inf)]
        bias = [bias_ref[j] for j in range(listed)] + [0.0]
        peak = functools.reduce(
            jnp.maximum,
            [jnp.max(s, axis=1, keepdims=True) - b for s, b in zip(scores, bias)],
        )
        weights = [jnp.exp2((s - (peak + b)) * factor) for s, b in zip(scores, bias)]
        total = sum(jnp.sum(w, axis=1, keepdims=True) for w in weights)
        mixed = sum(
            jnp.dot(
                w.astype(jnp.bfloat16),
                kv_ref[j, : w.shape[1], hd:],
                preferred_element_type=jnp.float32,
            )
            for j, w in enumerate(weights)
        )
        o_ref[part * tile : (part + 1) * tile, head * hd : (head + 1) * hd] = (
            mixed / total
        ).astype(o_ref.dtype)

    parts = [(head, part) for head in range(q_ref.shape[1] // hd) for part in range(2)]
    ahead = score(*parts[0])
    for i, part in enumerate(parts):
        scores = ahead
        if i + 1 < len(parts):
            ahead = score(*parts[i + 1])
        mix(*part, scores)


def attend(queries, near, bias, swapped):
    tokens, width = queries[0].shape
    blocks, size, both = near[0].shape
    hd = both // 2
    step = min(width, 4 * hd)
    work = tokens * blocks * size * (width // hd)
    shared = len(queries) == 2
    query_spec = pl.BlockSpec((tokens, step), lambda h: (0, h))
    scratch = [
        pltpu.VMEM(near[0].shape, near[0].dtype),
        pltpu.VMEM((tokens, step), jnp.bfloat16),
    ]
    return pl.pallas_call(
        functools.partial(attend_kernel, math.log2(math.e) / math.sqrt(hd), shared),
        grid=(width // step,),
        in_specs=[pl.BlockSpec(memory_space=pltpu.SMEM)] * 2
        + [query_spec] * len(queries)
        + [pl.BlockSpec(n.shape, lambda h: (0, 0, 0)) for n in near],
        out_specs=query_spec,
        out_shape=jax.ShapeDtypeStruct((tokens, width), jnp.bfloat16),
        scratch_shapes=scratch if shared else [],
        compiler_params=pltpu.CompilerParams(vmem_limit_bytes=VMEM),
        cost_estimate=pl.CostEstimate(flops=3910000000, bytes_accessed=1000, transcendentals=0),
        name="attend",
    )(bias, swapped, *queries, *near)


def project_kernel(parts, count, pieces, step, place_ref, *refs):
    attention, refs = refs[:parts], refs[parts:]
    arrays, refs = refs[:count], refs[count:]
    out_ref, weight_ref, left_ref, result_ref, weight_sems, left_sems, out_sems = refs
    steps = weight_ref.shape[1] // step

    def columns(n):
        return pl.ds(n * step, step)

    def weight_copy(n, i):
        array, row, depth = pieces[i]
        start = pl.multiple_of(place_ref[i], depth)
        return pltpu.make_async_copy(
            arrays[array].at[pl.ds(row, depth), columns(n)],
            weight_ref.at[pl.ds(start, depth), columns(n)],
            weight_sems.at[n, i],
        )

    wide = left_ref.shape[1] // parts
    lefts = [
        pltpu.make_async_copy(a, left_ref.at[:, pl.ds(i * wide, wide)], left_sems.at[i])
        for i, a in enumerate(attention)
    ]
    arriving = [started([weight_copy(0, i) for i in range(len(pieces))])]
    started(lefts)
    for n in range(1, steps):
        arriving.append(started([weight_copy(n, i) for i in range(len(pieces))]))
    waited(lefts)
    left = left_ref[...]
    leaving = []
    for n in range(steps):
        waited(arriving[n])
        total = jnp.dot(left, weight_ref[:, columns(n)], preferred_element_type=jnp.float32)
        result_ref[:, columns(n)] = total.astype(result_ref.dtype)
        leaving += started(
            [
                pltpu.make_async_copy(
                    result_ref.at[:, columns(n)], out_ref.at[:, columns(n)], out_sems.at[n]
                )
            ]
        )
    waited(leaving)


def project(attention, places, pieces):
    tokens = attention[0].shape[0]
    width = pieces[0][0].shape[1]
    arrays, held = [], []
    for array, row, depth in pieces:
        known = [i for i, other in enumerate(arrays) if other is array]
        if not known:
            arrays.append(array)
        held.append((known[0] if known else len(arrays) - 1, row, depth))
    rows = sum(depth for _, _, depth in held)
    step = min(1024, width)
    anywhere = pl.BlockSpec(memory_space=pl.ANY)
    return pl.pallas_call(
        functools.partial(project_kernel, len(attention), len(arrays), held, step),
        in_specs=[pl.BlockSpec(memory_space=pltpu.SMEM)]
        + [anywhere] * (len(attention) + len(arrays)),
        out_specs=anywhere,
        out_shape=jax.ShapeDtypeStruct((tokens, width), attention[0].dtype),
        scratch_shapes=[
            pltpu.VMEM((rows, width), arrays[0].dtype),
            pltpu.VMEM((tokens, rows), attention[0].dtype),
            pltpu.VMEM((tokens, width), attention[0].dtype),
            pltpu.SemaphoreType.DMA((width // step, len(held))),
            pltpu.SemaphoreType.DMA((len(attention),)),
            pltpu.SemaphoreType.DMA((width // step,)),
        ],
        compiler_params=pltpu.CompilerParams(vmem_limit_bytes=VMEM),
        cost_estimate=pl.CostEstimate(
            flops=2 * tokens * rows * width,
            bytes_accessed=2 * (rows + tokens) * width + 2 * tokens * rows,
            transcendentals=0,
        ),
        name="project",
    )(places, *attention, *arrays)


def ring_device(hidden_states, query_weight, output_weight, keys, values, block_lists):
    devices = lax.axis_size("ctx")
    chips = devices // 2
    half = chips // 2
    ring = list(range(0, chips, 2)) + list(range(chips - 1, 0, -2))
    at = {chip: i for i, chip in enumerate(ring)}
    depth, width = query_weight.shape
    size, head_size = keys.shape

    def pairs(step):
        return [
            (2 * p + c, 2 * ring[(at[p] + step) % chips] + c) for p in range(chips) for c in (0, 1)
        ]

    ahead, back = pairs(1), pairs(-1)

    def send(array, to):
        return lax.ppermute(array, "ctx", to)

    def swap(array):
        return send(array, [(d, d ^ 1) for d in range(devices)])

    def cross(array):
        return lax.ppermute(array, "groups", [(0, 1), (1, 0)])

    def held_back(array, *until):
        return lax.optimization_barrier((array, *until))[0]

    distances = [0] + [d for s in range(1, half) for d in (-s, s)] + [half]
    me, plane = lax.axis_index("ctx"), lax.axis_index("groups")
    chip, core = me // 2, me % 2
    here = jnp.where(chip % 2 == 0, chip // 2, chips - 1 - chip // 2)
    order = (here + jnp.asarray(distances, jnp.int32) + chips) % chips
    order = jnp.where(order < half, 2 * order, 2 * (chips - 1 - order) + 1)
    lists = lax.dynamic_slice_in_dim(block_lists, 2 * chip, 2, 0)
    lists = jnp.where(core == 0, lists, lists[::-1])
    listed = lists.shape[1]
    bias = jnp.where(lists[0] < me, 0.0, jnp.inf).astype(jnp.float32)
    swapped = (lists[0] % 2 != core).astype(jnp.int32)
    held_at = jnp.argmax(order == lists[:, :, None] // 2, axis=2).astype(jnp.int32).reshape(-1)
    plane = jnp.reshape(plane, (1,)).astype(jnp.int32)
    places = 2 * order + core
    early, late = 2 * half - 3, 2 * half
    scalars = {
        (which, when): jnp.concatenate([plane if which == 0 else 1 - plane, places[span], held_at])
        for which in (0, 1)
        for when, span in enumerate((slice(0, early), slice(early, late)))
    }
    rows = output_weight.shape[0]
    cut = rows // 2
    row_of = 2 * order[:, None] + (core + jnp.arange(2, dtype=jnp.int32)) % 2
    row_of = ((row_of + chips * plane) % devices * rows).reshape(-1)
    row_of = jnp.concatenate([row_of, row_of[-2:] + cut])
    bias, swapped, row_of, scalars = lax.optimization_barrier((bias, swapped, row_of, scalars))

    hidden = (swap(hidden_states), hidden_states)
    own = pack(plane, query_weight, keys, values)

    def part(which, found, when, totals, **more):
        spans = distances[:early] if when == 0 else distances[early:]
        pieces = [(query_weight, 0) if d == 0 else found[d] for d in spans]
        return query(
            hidden, scalars[which, when], query_weight, pieces, depth, width // 2, totals, **more
        )

    near, crossed = {}, {}
    down, up = own, own
    behind = [bias, swapped, row_of, scalars[0, 0]]
    for step in range(1, half):
        down, up = send(down, ahead), send(up, back)
        over = jnp.concatenate([down[:, : width // 2], up[:, : width // 2]], 0)
        over = cross(over) if step < half - 1 else over
        near[-step], near[step] = (down, 0), (up, 0)
        crossed[-step], crossed[step] = (over, 0), (over, 1)
        if step == half - 1:
            first = part(0, near, 0, ())
            behind = [*first, crossed[step - 2][0]]
        down, up = held_back(down, *behind), held_back(up, *behind)
        behind = []
    down, up = send(down[: depth // 2], ahead), send(up[depth // 2 :], back)
    far = jnp.concatenate([down, up], 0)
    near[half] = (far, 0)
    over = cross(jnp.concatenate([over, far[:, : width // 2]], 0))
    for i, distance in enumerate((1 - half, half - 1, half)):
        crossed[distance] = (over, i)
    second = part(1, crossed, 0, ())
    last = [down, up, *second]
    blocks = [(own, 0)] + [near[d] for d in distances[1:]]
    block = (size, 2 * head_size)
    theirs, ours, picked, given = part(
        0, near, 1, first, blocks=blocks, listed=listed, block=block
    )
    queries = [(ours, swap(theirs))]
    picked = (picked, swap(given))

    pieces = [(output_weight, 0, rows), (swap(output_weight), 0, rows)]
    down, up = held_back(output_weight, *last), held_back(output_weight, *last)
    attention = []
    behind = [pieces[1][0], given]
    for step in range(1, half):
        came = [down, up]
        down, up = send(down, ahead), send(up, back)
        pair = jnp.concatenate([down, up], 0)
        if step == 2:
            attention.append(attend(queries[0], picked, held_back(bias, *came), swapped))
            behind.append(attention[0])
        if step == half - 1:
            second = lax.optimization_barrier((*second, *attention, *came))[:2]
            theirs, ours = part(1, crossed, 1, second)
            attention.append(attend((ours, swap(theirs)), picked, bias, swapped))
        other = swap(pair)
        pieces += [(down, 0, rows), (other, 0, rows), (up, 0, rows), (other, rows, rows)]
        down, up = held_back(down, *behind), held_back(up, *behind)
        behind = [other]
    down, up = send(down[:cut], ahead), send(up[cut:], back)
    got = [swap(held_back(x, attention[-1])) for x in (down, up)]
    pieces += [(down, 0, cut), (got[0], 0, cut), (up, 0, cut), (got[1], 0, cut)]
    return project(attention, row_of, pieces)


def per_device(hidden_states, query_weight, output_weight, keys, values, block_lists):
    devices = lax.axis_size("ctx")
    head_size = keys.shape[1]
    piece_rows = BLOCK // devices
    me = lax.axis_index("ctx")
    total = jnp.dot(
        hidden_states,
        lax.all_gather(query_weight, "ctx", axis=0, tiled=True),
        preferred_element_type=jnp.float32,
    )
    queries = total.astype(jnp.bfloat16)
    near = jnp.concatenate([keys, values], 1)
    spread = lax.all_to_all(near[None], "ctx", split_axis=1, concat_axis=0, tiled=True)
    listed = jnp.take(spread, block_lists, axis=0).reshape(
        devices, TOPK, piece_rows, 2 * head_size
    )
    got = lax.all_to_all(listed, "ctx", split_axis=0, concat_axis=2, tiled=True)
    picked = jnp.concatenate([got.reshape(TOPK, BLOCK, 2 * head_size), near[None]], 0)
    mine = lax.dynamic_index_in_dim(block_lists, me, 0, keepdims=False)
    bias = jnp.where(mine < me, 0.0, jnp.inf).astype(jnp.float32)
    attention = attend((queries,), (picked,), bias, jnp.zeros_like(mine))
    projected = jnp.dot(
        attention,
        lax.all_gather(output_weight, "ctx", axis=0, tiled=True),
        preferred_element_type=jnp.float32,
    )
    return projected.astype(jnp.bfloat16)


def solution(mesh):
    in_specs = (
        P(("groups", "ctx"), None),
        P("ctx", None),
        P("ctx", None),
        P(("groups", "ctx"), None),
        P(("groups", "ctx"), None),
        P("groups", None),
    )
    out_specs = P(("groups", "ctx"), None)
    step_by_step = mesh.shape["ctx"] <= 2 * RING_CHIPS and mesh.shape["groups"] == 2
    return jax.shard_map(
        ring_device if step_by_step else per_device,
        mesh=mesh,
        in_specs=in_specs,
        out_specs=out_specs,
        check_vma=False,
    )
```

```python
import functools
import math

import jax
import jax.numpy as jnp
from jax import lax
from jax.experimental import pallas as pl
from jax.experimental.pallas import tpu as pltpu
from jax.sharding import PartitionSpec as P

BLOCK = 512
TOPK = 3
RING_CHIPS = 8
MIB = 2**20
VMEM = 28 * MIB


def pack_kernel(plane_ref, weight_ref, keys_ref, values_ref, out_ref):
    depth, width = weight_ref.shape
    head_size = keys_ref.shape[1]
    out_ref[:, :width] = weight_ref[...]
    for i, rows in enumerate(range(0, keys_ref.shape[0], depth)):
        at = width + 2 * i * head_size
        out_ref[:, at : at + head_size] = keys_ref[rows : rows + depth, :]
        out_ref[:, at + head_size : at + 2 * head_size] = values_ref[rows : rows + depth, :]


def pack(plane, weight, keys, values):
    depth, width = weight.shape
    size, head_size = keys.shape
    wide = width // 2 + 2 * head_size * (size // depth)
    return pl.pallas_call(
        pack_kernel,
        grid_spec=pltpu.PrefetchScalarGridSpec(
            num_scalar_prefetch=1,
            grid=(1,),
            in_specs=[
                pl.BlockSpec((depth, width // 2), lambda i, plane: (0, plane[0])),
                pl.BlockSpec(keys.shape, lambda i, plane: (0, 0)),
                pl.BlockSpec(values.shape, lambda i, plane: (0, 0)),
            ],
            out_specs=pl.BlockSpec((depth, wide), lambda i, plane: (0, 0)),
        ),
        out_shape=jax.ShapeDtypeStruct((depth, wide), weight.dtype),
        compiler_params=pltpu.CompilerParams(vmem_limit_bytes=60 * MIB),
        name="pack",
    )(plane, weight, keys, values)


def started(copies):
    for copy in copies:
        copy.start()
    return copies


def waited(copies):
    for copy in copies:
        copy.wait()


def query_kernel(depth, pieces, summed, blocks, scalar_ref, *refs):
    count = len(pieces)
    arrays, refs = refs[: 1 + max(p for p, _ in pieces + blocks)], refs[1 + max(p for p, _ in pieces + blocks) :]
    hidden, refs = refs[:2], refs[2:]
    totals, refs = (refs[:2], refs[2:]) if summed else ((), refs)
    outs, refs = refs[:2], refs[2:]
    near, refs = (refs[:2], refs[2:]) if blocks else ((), refs)
    weight_ref, hidden_ref, total_ref, weight_sems, hidden_sems, total_sems, out_sems = refs[:7]
    tokens, width = total_ref.shape[1:]

    def weight_copy(i):
        array, row = pieces[i]
        wide = array == 0
        start = pl.multiple_of(scalar_ref[0] * width, width) if wide else 0
        return pltpu.make_async_copy(
            arrays[array].at[pl.ds(row * depth, depth), pl.ds(start, width)],
            weight_ref.at[pl.ds(i * depth, depth)],
            weight_sems.at[i],
        )

    def hidden_copy(side, i):
        start = pl.multiple_of(scalar_ref[1 + i] * depth, depth)
        return pltpu.make_async_copy(
            hidden[side].at[:, pl.ds(start, depth)],
            hidden_ref.at[side, :, pl.ds(i * depth, depth)],
            hidden_sems.at[side, i],
        )

    def near_copies(source, target, slot):
        array, row = source
        both, size = target.shape[2], target.shape[1]
        return [
            pltpu.make_async_copy(
                arrays[array].at[pl.ds(row * depth, depth), pl.ds(width + h * both, both)],
                target.at[slot, pl.ds(h * depth, depth)],
                refs[7].at[0 if target is near[0] else 1, slot, h],
            )
            for h in range(size // depth)
        ]

    weights = started([weight_copy(i) for i in range(count)])
    lefts = [started([hidden_copy(side, i) for i in range(count)]) for side in range(2)]
    added = []
    for side in range(2 if summed else 0):
        added.append(
            started(
                [pltpu.make_async_copy(totals[side], total_ref.at[side], total_sems.at[side])]
            )
        )
    if blocks:
        listed = near[1].shape[0]
        for side in range(2):
            for j in range(listed):
                for s, source in enumerate(blocks):

                    @pl.when(scalar_ref[1 + count + side * listed + j] == s)
                    def _(side=side, j=j, source=source):
                        started(near_copies(source, near[side], j))

        started(near_copies(blocks[0], near[0], listed))
    waited(weights)
    sent = []
    for side in range(2):
        waited(lefts[side])
        total = jnp.dot(hidden_ref[side], weight_ref[...], preferred_element_type=jnp.float32)
        if summed:
            waited(added[side])
            total += total_ref[side]
        total_ref[side] = total
        sent += started(
            [pltpu.make_async_copy(total_ref.at[side], outs[side], out_sems.at[side])]
        )
    if blocks:
        for side in range(2):
            for j in range(listed + 1 - side):
                waited(near_copies(blocks[0], near[side], j))
    waited(sent)


def query(hidden, scalars, weight, pieces, depth, width, totals, blocks=(), listed=0, block=None):
    tokens = hidden[0].shape[0]
    arrays = [weight]

    def index(array):
        for i, known in enumerate(arrays):
            if known is array:
                return i
        arrays.append(array)
        return len(arrays) - 1

    where = [(index(array), row) for array, row in pieces]
    held = [(index(array), row) for array, row in blocks]
    count = len(pieces)
    out_shape = [jax.ShapeDtypeStruct((tokens, width), jnp.float32)] * 2
    scratch = [
        pltpu.VMEM((count * depth, width), weight.dtype),
        pltpu.VMEM((2, tokens, count * depth), weight.dtype),
        pltpu.VMEM((2, tokens, width), jnp.float32),
        pltpu.SemaphoreType.DMA((count,)),
        pltpu.SemaphoreType.DMA((2, count)),
        pltpu.SemaphoreType.DMA((2,)),
        pltpu.SemaphoreType.DMA((2,)),
    ]
    if blocks:
        out_shape += [
            jax.ShapeDtypeStruct((listed + 1,) + block, weight.dtype),
            jax.ShapeDtypeStruct((listed,) + block, weight.dtype),
        ]
        scratch.append(pltpu.SemaphoreType.DMA((2, listed + 1, block[0] // depth)))
    operands = [*arrays, *hidden, *totals]
    anywhere = pl.BlockSpec(memory_space=pl.ANY)
    return pl.pallas_call(
        functools.partial(query_kernel, depth, where, bool(totals), held),
        in_specs=[pl.BlockSpec(memory_space=pltpu.SMEM)] + [anywhere] * len(operands),
        out_specs=[anywhere] * 2 + [pl.BlockSpec(memory_space=pltpu.VMEM)] * (len(out_shape) - 2),
        out_shape=out_shape,
        scratch_shapes=scratch,
        compiler_params=pltpu.CompilerParams(vmem_limit_bytes=VMEM),
        cost_estimate=pl.CostEstimate(flops=1955000000, bytes_accessed=1000, transcendentals=0),
        name="query",
    )(scalars, *operands)


def attend_kernel(factor, shared, bias_ref, swap_ref, *refs):
    if shared:
        q_own_ref, q_got_ref, near_ref, got_ref, o_ref, kv_ref, q_ref = refs
        listed = got_ref.shape[0]
        q_ref[...] = (q_own_ref[...] + q_got_ref[...]).astype(q_ref.dtype)
        kv_ref[listed] = near_ref[listed]
        for j in range(listed):

            @pl.when(swap_ref[j] == 0)
            def _(j=j):
                kv_ref[j] = near_ref[j]

            @pl.when(swap_ref[j] != 0)
            def _(j=j):
                kv_ref[j] = got_ref[j]

    else:
        q_ref, kv_ref, o_ref = refs
    blocks, size, both = kv_ref.shape
    hd, listed, tile = both // 2, blocks - 1, size // 2
    across = (((1,), (1,)), ((), ()))

    def score(head, part):
        q = q_ref[part * tile : (part + 1) * tile, head * hd : (head + 1) * hd]
        spans = [(j, size) for j in range(listed)] + [(listed, tile * (part + 1))]
        return [
            lax.dot_general(
                q, kv_ref[j, :seen, :hd], across, preferred_element_type=jnp.float32
            )
            for j, seen in spans
        ]

    def mix(head, part, scores):
        at_query = lax.broadcasted_iota(jnp.int32, scores[-1].shape, 0) + part * tile
        at_key = lax.broadcasted_iota(jnp.int32, scores[-1].shape, 1)
        scores = scores[:-1] + [jnp.where(at_query >= at_key, scores[-1], -jnp.inf)]
        bias = [bias_ref[j] for j in range(listed)] + [0.0]
        peak = functools.reduce(
            jnp.maximum,
            [jnp.max(s, axis=1, keepdims=True) - b for s, b in zip(scores, bias)],
        )
        weights = [jnp.exp2((s - (peak + b)) * factor) for s, b in zip(scores, bias)]
        total = sum(jnp.sum(w, axis=1, keepdims=True) for w in weights)
        mixed = sum(
            jnp.dot(
                w.astype(jnp.bfloat16),
                kv_ref[j, : w.shape[1], hd:],
                preferred_element_type=jnp.float32,
            )
            for j, w in enumerate(weights)
        )
        o_ref[part * tile : (part + 1) * tile, head * hd : (head + 1) * hd] = (
            mixed / total
        ).astype(o_ref.dtype)

    parts = [(head, part) for head in range(q_ref.shape[1] // hd) for part in range(2)]
    ahead = score(*parts[0])
    for i, part in enumerate(parts):
        scores = ahead
        if i + 1 < len(parts):
            ahead = score(*parts[i + 1])
        mix(*part, scores)


def attend(queries, near, bias, swapped):
    tokens, width = queries[0].shape
    blocks, size, both = near[0].shape
    hd = both // 2
    step = min(width, 4 * hd)
    work = tokens * blocks * size * (width // hd)
    shared = len(queries) == 2
    query_spec = pl.BlockSpec((tokens, step), lambda h: (0, h))
    scratch = [
        pltpu.VMEM(near[0].shape, near[0].dtype),
        pltpu.VMEM((tokens, step), jnp.bfloat16),
    ]
    return pl.pallas_call(
        functools.partial(attend_kernel, math.log2(math.e) / math.sqrt(hd), shared),
        grid=(width // step,),
        in_specs=[pl.BlockSpec(memory_space=pltpu.SMEM)] * 2
        + [query_spec] * len(queries)
        + [pl.BlockSpec(n.shape, lambda h: (0, 0, 0)) for n in near],
        out_specs=query_spec,
        out_shape=jax.ShapeDtypeStruct((tokens, width), jnp.bfloat16),
        scratch_shapes=scratch if shared else [],
        compiler_params=pltpu.CompilerParams(vmem_limit_bytes=VMEM),
        cost_estimate=pl.CostEstimate(flops=3910000000, bytes_accessed=1000, transcendentals=0),
        name="attend",
    )(bias, swapped, *queries, *near)


def project_kernel(parts, count, pieces, step, place_ref, *refs):
    attention, refs = refs[:parts], refs[parts:]
    arrays, refs = refs[:count], refs[count:]
    out_ref, weight_ref, left_ref, result_ref, weight_sems, left_sems, out_sems = refs
    steps = weight_ref.shape[1] // step

    def columns(n):
        return pl.ds(n * step, step)

    def weight_copy(n, i):
        array, row, depth = pieces[i]
        start = pl.multiple_of(place_ref[i], depth)
        return pltpu.make_async_copy(
            arrays[array].at[pl.ds(row, depth), columns(n)],
            weight_ref.at[pl.ds(start, depth), columns(n)],
            weight_sems.at[n, i],
        )

    wide = left_ref.shape[1] // parts
    lefts = [
        pltpu.make_async_copy(a, left_ref.at[:, pl.ds(i * wide, wide)], left_sems.at[i])
        for i, a in enumerate(attention)
    ]
    arriving = [started([weight_copy(0, i) for i in range(len(pieces))])]
    started(lefts)
    for n in range(1, steps):
        arriving.append(started([weight_copy(n, i) for i in range(len(pieces))]))
    waited(lefts)
    left = left_ref[...]
    leaving = []
    for n in range(steps):
        waited(arriving[n])
        total = jnp.dot(left, weight_ref[:, columns(n)], preferred_element_type=jnp.float32)
        result_ref[:, columns(n)] = total.astype(result_ref.dtype)
        leaving += started(
            [
                pltpu.make_async_copy(
                    result_ref.at[:, columns(n)], out_ref.at[:, columns(n)], out_sems.at[n]
                )
            ]
        )
    waited(leaving)


def project(attention, places, pieces):
    tokens = attention[0].shape[0]
    width = pieces[0][0].shape[1]
    arrays, held = [], []
    for array, row, depth in pieces:
        known = [i for i, other in enumerate(arrays) if other is array]
        if not known:
            arrays.append(array)
        held.append((known[0] if known else len(arrays) - 1, row, depth))
    rows = sum(depth for _, _, depth in held)
    step = min(1024, width)
    anywhere = pl.BlockSpec(memory_space=pl.ANY)
    return pl.pallas_call(
        functools.partial(project_kernel, len(attention), len(arrays), held, step),
        in_specs=[pl.BlockSpec(memory_space=pltpu.SMEM)]
        + [anywhere] * (len(attention) + len(arrays)),
        out_specs=anywhere,
        out_shape=jax.ShapeDtypeStruct((tokens, width), attention[0].dtype),
        scratch_shapes=[
            pltpu.VMEM((rows, width), arrays[0].dtype),
            pltpu.VMEM((tokens, rows), attention[0].dtype),
            pltpu.VMEM((tokens, width), attention[0].dtype),
            pltpu.SemaphoreType.DMA((width // step, len(held))),
            pltpu.SemaphoreType.DMA((len(attention),)),
            pltpu.SemaphoreType.DMA((width // step,)),
        ],
        compiler_params=pltpu.CompilerParams(vmem_limit_bytes=VMEM),
        cost_estimate=pl.CostEstimate(
            flops=2 * tokens * rows * width,
            bytes_accessed=2 * (rows + tokens) * width + 2 * tokens * rows,
            transcendentals=0,
        ),
        name="project",
    )(places, *attention, *arrays)


def ring_device(hidden_states, query_weight, output_weight, keys, values, block_lists):
    devices = lax.axis_size("ctx")
    chips = devices // 2
    half = chips // 2
    ring = list(range(0, chips, 2)) + list(range(chips - 1, 0, -2))
    at = {chip: i for i, chip in enumerate(ring)}
    depth, width = query_weight.shape
    size, head_size = keys.shape

    def pairs(step):
        return [
            (2 * p + c, 2 * ring[(at[p] + step) % chips] + c) for p in range(chips) for c in (0, 1)
        ]

    ahead, back = pairs(1), pairs(-1)

    def send(array, to):
        return lax.ppermute(array, "ctx", to)

    def swap(array):
        return send(array, [(d, d ^ 1) for d in range(devices)])

    def cross(array):
        return lax.ppermute(array, "groups", [(0, 1), (1, 0)])

    def held_back(array, *until):
        return lax.optimization_barrier((array, *until))[0]

    distances = [0] + [d for s in range(1, half) for d in (-s, s)] + [half]
    me, plane = lax.axis_index("ctx"), lax.axis_index("groups")
    chip, core = me // 2, me % 2
    here = jnp.where(chip % 2 == 0, chip // 2, chips - 1 - chip // 2)
    order = (here + jnp.asarray(distances, jnp.int32) + chips) % chips
    order = jnp.where(order < half, 2 * order, 2 * (chips - 1 - order) + 1)
    lists = lax.dynamic_slice_in_dim(block_lists, 2 * chip, 2, 0)
    lists = jnp.where(core == 0, lists, lists[::-1])
    listed = lists.shape[1]
    bias = jnp.where(lists[0] < me, 0.0, jnp.inf).astype(jnp.float32)
    swapped = (lists[0] % 2 != core).astype(jnp.int32)
    held_at = jnp.argmax(order == lists[:, :, None] // 2, axis=2).astype(jnp.int32).reshape(-1)
    plane = jnp.reshape(plane, (1,)).astype(jnp.int32)
    places = 2 * order + core
    early, late = 2 * half - 3, 2 * half
    scalars = {
        (which, when): jnp.concatenate([plane if which == 0 else 1 - plane, places[span], held_at])
        for which in (0, 1)
        for when, span in enumerate((slice(0, early), slice(early, late)))
    }
    rows = output_weight.shape[0]
    cut = rows // 2
    row_of = 2 * order[:, None] + (core + jnp.arange(2, dtype=jnp.int32)) % 2
    row_of = ((row_of + chips * plane) % devices * rows).reshape(-1)
    row_of = jnp.concatenate([row_of, row_of[-2:] + cut])
    bias, swapped, row_of, scalars = lax.optimization_barrier((bias, swapped, row_of, scalars))

    hidden = (swap(hidden_states), hidden_states)
    own = pack(plane, query_weight, keys, values)

    def part(which, found, when, totals, **more):
        spans = distances[:early] if when == 0 else distances[early:]
        pieces = [(query_weight, 0) if d == 0 else found[d] for d in spans]
        return query(
            hidden, scalars[which, when], query_weight, pieces, depth, width // 2, totals, **more
        )

    near, crossed = {}, {}
    down, up = own, own
    behind = [bias, swapped, row_of, scalars[0, 0]]
    for step in range(1, half):
        down, up = send(down, ahead), send(up, back)
        over = jnp.concatenate([down[:, : width // 2], up[:, : width // 2]], 0)
        over = cross(over) if step < half - 1 else over
        near[-step], near[step] = (down, 0), (up, 0)
        crossed[-step], crossed[step] = (over, 0), (over, 1)
        if step == half - 1:
            first = part(0, near, 0, ())
            behind = [*first, crossed[step - 2][0]]
        down, up = held_back(down, *behind), held_back(up, *behind)
        behind = []
    sent = [down, up]
    down, up = send(down[: depth // 2], ahead), send(up[depth // 2 :], back)
    far = jnp.concatenate([down, up], 0)
    near[half] = (far, 0)
    over = cross(jnp.concatenate([over, far[:, : width // 2]], 0))
    for i, distance in enumerate((1 - half, half - 1, half)):
        crossed[distance] = (over, i)
    second = part(1, crossed, 0, ())
    last = [*sent, *second]
    blocks = [(own, 0)] + [near[d] for d in distances[1:]]
    block = (size, 2 * head_size)
    theirs, ours, picked, given = part(
        0, near, 1, first, blocks=blocks, listed=listed, block=block
    )
    queries = [(ours, swap(theirs))]
    picked = (picked, swap(given))

    pieces = [(output_weight, 0, rows), (swap(output_weight), 0, rows)]
    down, up = held_back(output_weight, *last), held_back(output_weight, *last)
    attention = []
    behind = [pieces[1][0], given]
    for step in range(1, half):
        came = [down, up]
        down, up = send(down, ahead), send(up, back)
        pair = jnp.concatenate([down, up], 0)
        if step == 2:
            attention.append(attend(queries[0], picked, held_back(bias, *came), swapped))
            behind.append(attention[0])
        if step == half - 1:
            second = lax.optimization_barrier((*second, *attention, *came))[:2]
            theirs, ours = part(1, crossed, 1, second)
            attention.append(attend((ours, swap(theirs)), picked, bias, swapped))
        other = swap(pair)
        pieces += [(down, 0, rows), (other, 0, rows), (up, 0, rows), (other, rows, rows)]
        down, up = held_back(down, *behind), held_back(up, *behind)
        behind = [other]
    down, up = send(down[:cut], ahead), send(up[cut:], back)
    got = [swap(held_back(x, attention[-1])) for x in (down, up)]
    pieces += [(down, 0, cut), (got[0], 0, cut), (up, 0, cut), (got[1], 0, cut)]
    return project(attention, row_of, pieces)


def per_device(hidden_states, query_weight, output_weight, keys, values, block_lists):
    devices = lax.axis_size("ctx")
    head_size = keys.shape[1]
    piece_rows = BLOCK // devices
    me = lax.axis_index("ctx")
    total = jnp.dot(
        hidden_states,
        lax.all_gather(query_weight, "ctx", axis=0, tiled=True),
        preferred_element_type=jnp.float32,
    )
    queries = total.astype(jnp.bfloat16)
    near = jnp.concatenate([keys, values], 1)
    spread = lax.all_to_all(near[None], "ctx", split_axis=1, concat_axis=0, tiled=True)
    listed = jnp.take(spread, block_lists, axis=0).reshape(
        devices, TOPK, piece_rows, 2 * head_size
    )
    got = lax.all_to_all(listed, "ctx", split_axis=0, concat_axis=2, tiled=True)
    picked = jnp.concatenate([got.reshape(TOPK, BLOCK, 2 * head_size), near[None]], 0)
    mine = lax.dynamic_index_in_dim(block_lists, me, 0, keepdims=False)
    bias = jnp.where(mine < me, 0.0, jnp.inf).astype(jnp.float32)
    attention = attend((queries,), (picked,), bias, jnp.zeros_like(mine))
    projected = jnp.dot(
        attention,
        lax.all_gather(output_weight, "ctx", axis=0, tiled=True),
        preferred_element_type=jnp.float32,
    )
    return projected.astype(jnp.bfloat16)


def solution(mesh):
    in_specs = (
        P(("groups", "ctx"), None),
        P("ctx", None),
        P("ctx", None),
        P(("groups", "ctx"), None),
        P(("groups", "ctx"), None),
        P("groups", None),
    )
    out_specs = P(("groups", "ctx"), None)
    step_by_step = mesh.shape["ctx"] <= 2 * RING_CHIPS and mesh.shape["groups"] == 2
    return jax.shard_map(
        ring_device if step_by_step else per_device,
        mesh=mesh,
        in_specs=in_specs,
        out_specs=out_specs,
        check_vma=False,
    )
```
